256 devices in a mesh: lat: 8 (over x_hi, y), lon: 32 (over z, x_lo, core).
Axes of the slice: x: 4 (x_hi: 2, x_lo: 2; x = x_hi * 2 + x_lo), y: 4, z: 8, core: 2. Of those that a mesh axis runs over, the one named last changes fastest.
Arguments:
- fields: bfloat16 [2, 64, 768, 256], P(None, 'lat', 'lon'), may hold values from -6 to 6
- filters: bfloat16 [64, 5, 9, 4], replicated, may hold values from -0.875 to 0.875
- lon_width: int32 [64], replicated, may hold values from 1 to 4, as said below
- disco_weight: bfloat16 [4, 256, 256], replicated, may hold values from -0.1875 to 0.1875
- up_weight: bfloat16 [256, 512], replicated, may hold values from -0.375 to 0.375
- down_weight: bfloat16 [512, 256], replicated, may hold values from -0.25 to 0.25
- cotangent: bfloat16 [2, 64, 768, 256], P(None, 'lat', 'lon'), may hold values from -6 to 6
Outputs:
- output: bfloat16 [2, 64, 768, 256], P(None, 'lat', 'lon')
- back_fields: bfloat16 [2, 64, 768, 256], P(None, 'lat', 'lon')
- grad_disco: float32 [4, 256, 256], replicated
- grad_up: float32 [256, 512], replicated
- grad_down: float32 [512, 256], replicated
The draws below stay inside these ranges and needn't reach their ends.
Inputs may be any that keep to these rules, and one draw needn't show every extreme that they name: lon_width equals 4 at the 2 rows nearest each pole.
All inputs are finite; a program needn't handle non-finite values.
Results may differ from the reference program's by a relative error of at most 0.013.
Values may be sent and summed in bfloat16 or wider, within the bound.
A program may use at most 128 MiB of HBM per device.

```python
import jax
import jax.numpy as jnp
from jax import lax

C = 256
FF = 512
K = 4
R = 2
HW = 4
M = 2
NLAT = 64
NLON = 768


def draw_lon_width(key, part):
    key = jax.random.fold_in(key, 11)
    widths = jax.random.randint(key, (NLAT,), 1, HW + 1)
    rows_all = jnp.arange(NLAT)
    polar = (rows_all < R) | (rows_all >= NLAT - R)
    return jnp.where(polar, HW, widths).astype(jnp.int32)


def steps_of(stream_key, dims, shards, low, high):
    factor_of = 1.0
    for dim, blocks in shards:
        heights = jax.random.uniform(jax.random.fold_in(jax.random.fold_in(stream_key, 6), dim), (blocks,), jnp.float32, low / len(shards), high / len(shards))
        factor_of = factor_of * jnp.repeat(jnp.exp(heights), dims[dim] // blocks).reshape((-1,) + (1,) * (len(dims) - 1 - dim))
    return factor_of


def gaussian(rng, dims, scale, most, split=(), kind=jnp.bfloat16):
    drawn = scale * jax.random.normal(rng, dims, jnp.float32)
    if split:
        drawn = drawn * steps_of(rng, dims, split, -0.22, 0.18)
    return jnp.clip(drawn, -most, most).astype(kind)


def setup_inputs(seed: int = 0) -> dict:
    key_list = jax.random.split(jax.random.key(seed), 8)
    return {
        "fields": gaussian(key_list[0], (M, NLAT, NLON, C), 1.0, 6.0, ((1, 8), (2, 32))),
        "filters": gaussian(key_list[1], (NLAT, 2 * R + 1, 2 * HW + 1, K), 0.15, 0.875),
        "lon_width": draw_lon_width(jax.random.fold_in(key_list[7], 71), 0),
        "disco_weight": gaussian(key_list[3], (K, C, C), (K * C) ** -0.5, 0.1875),
        "up_weight": gaussian(key_list[4], (C, FF), C ** -0.5, 0.375),
        "down_weight": gaussian(key_list[5], (FF, C), FF ** -0.5, 0.25),
        "cotangent": gaussian(key_list[6], (M, NLAT, NLON, C), 1.0, 6.0, ((1, 8), (2, 32))),
    }


GELU_SCALE = 0.7978845608028654
GELU_CUBE = 0.044715


def gelu_value(pre):
    inner = jnp.tanh(GELU_SCALE * (pre + GELU_CUBE * pre * pre * pre))
    return 0.5 * pre * (1.0 + inner)


def gelu_slope(pre):
    inner = jnp.tanh(GELU_SCALE * (pre + GELU_CUBE * pre * pre * pre))
    return 0.5 * (1.0 + inner) + 0.5 * pre * (1.0 - inner * inner) * GELU_SCALE * (1.0 + 3.0 * GELU_CUBE * pre * pre)


def masked_filter(filters, lon_width):
    reach_cols = (filters.shape[2] - 1) // 2
    offsets = jnp.abs(jnp.arange(filters.shape[2], dtype=jnp.int32) - reach_cols).astype(jnp.int32)
    keep = offsets[None, :] <= lon_width[:, None]
    return jnp.where(keep[:, None, :, None], filters, jnp.zeros_like(filters))


def pad_member(member):
    pads = [(R, R)] + [(0, 0)] * (member.ndim - 1)
    framed = jnp.pad(member, pads)
    return jnp.concatenate([framed[:, NLON - HW:], framed, framed[:, :HW]], axis=1)


def forward_member(member, weights):
    padded = pad_member(member)
    total = jnp.zeros((NLAT, NLON, K, C), jnp.float32)
    for row_tap in range(2 * R + 1):
        window = jnp.stack([padded[row_tap:row_tap + NLAT, col_tap:col_tap + NLON] for col_tap in range(2 * HW + 1)], axis=2)
        coeff = weights[:, row_tap].astype(jnp.float32)
        total = total + jnp.einsum('ijdc,idk->ijkc', window.astype(jnp.float32), coeff)
    return total.astype(jnp.bfloat16)


def backward_member(member, framed_weights):
    padded = pad_member(member)
    total = jnp.zeros((NLAT, NLON, C), jnp.float32)
    for row_tap in range(2 * R + 1):
        start = 2 * R - row_tap
        coeff = framed_weights[start:start + NLAT, row_tap].astype(jnp.float32)
        for level in range(K):
            window = jnp.stack([padded[start:start + NLAT, 2 * HW - col_tap:2 * HW - col_tap + NLON, level] for col_tap in range(2 * HW + 1)], axis=2)
            total = total + jnp.einsum('ijdc,id->ijc', window.astype(jnp.float32), coeff[:, :, level])
    return total


def reference(fields, filters, lon_width, disco_weight, up_weight, down_weight, cotangent):
    weights = masked_filter(filters, lon_width)
    spread = lax.map(lambda member: forward_member(member, weights), fields)
    tokens = M * NLAT * NLON
    flat = spread.reshape(tokens, K * C)
    disco_flat = disco_weight.reshape(K * C, C)
    resid = (fields.reshape(tokens, C).astype(jnp.float32) + jnp.dot(flat, disco_flat, preferred_element_type=jnp.float32)).astype(jnp.bfloat16)
    pre = jnp.dot(resid, up_weight, preferred_element_type=jnp.float32)
    hidden = gelu_value(pre).astype(jnp.bfloat16)
    output = (resid.astype(jnp.float32) + jnp.dot(hidden, down_weight, preferred_element_type=jnp.float32)).astype(jnp.bfloat16)
    cot = cotangent.reshape(tokens, C)
    back_pre = (jnp.dot(cot, down_weight.T, preferred_element_type=jnp.float32) * gelu_slope(pre)).astype(jnp.bfloat16)
    grad_down = jnp.dot(hidden.T, cot, preferred_element_type=jnp.float32)
    grad_up = jnp.dot(resid.T, back_pre, preferred_element_type=jnp.float32)
    back_resid = (cot.astype(jnp.float32) + jnp.dot(back_pre, up_weight.T, preferred_element_type=jnp.float32)).astype(jnp.bfloat16)
    grad_disco = jnp.dot(flat.T, back_resid, preferred_element_type=jnp.float32).reshape(K, C, C)
    back_spread = jnp.dot(back_resid, disco_flat.T, preferred_element_type=jnp.float32).astype(jnp.bfloat16).reshape(M, NLAT, NLON, K, C)
    framed_weights = jnp.pad(weights, ((R, R), (0, 0), (0, 0), (0, 0)))
    spread_back = lax.map(lambda member: backward_member(member, framed_weights), back_spread)
    back_fields = (back_resid.reshape(M, NLAT, NLON, C).astype(jnp.float32) + spread_back).astype(jnp.bfloat16)
    return output.reshape(M, NLAT, NLON, C), back_fields, grad_disco, grad_up, grad_down
```

```python
import functools

import jax
import jax.numpy as jnp
import numpy as np
from jax import lax
from jax.experimental import pallas as pl
from jax.experimental.pallas import tpu as pltpu
from jax.sharding import PartitionSpec as P

GELU_SCALE = 0.7978845608028654
GELU_CUBE = 0.044715
MESH = pl.DeviceIdType.MESH
F32 = jnp.float32
BF16 = jnp.bfloat16

M, ROWS, CELLS, C, FF, K = 2, 8, 24, 256, 512, 4
NLAT = 64
A_TAPS, B_TAPS = 5, 9
PAIRS = ROWS // 2
TOK = M * ROWS * CELLS
BLOCK = 80
NK = 3 * BLOCK


def constants():
    sel_f = np.zeros((256, K * 256), np.float32)
    sel_b = np.zeros((256, K * 256), np.float32)
    for a in range(A_TAPS):
        for b in range(B_TAPS):
            for k in range(K):
                s = a * B_TAPS * K + b * K + k
                sel_f[s, k * 256 + a * 32 + b] = 1
                sel_b[s, k * 256 + (4 - a) * 32 + 8 - b] = 1
    perm = np.zeros((2, 256, 256), np.float32)
    for i2 in range(2):
        for a in range(A_TAPS):
            p, r2 = divmod(i2 + a, 2)
            for jj in range(32):
                if jj < 4:
                    col = p * BLOCK + 48 + r2 * 4 + jj
                elif jj < 28:
                    col = p * BLOCK + r2 * CELLS + jj - 4
                else:
                    col = p * BLOCK + 64 + r2 * 4 + jj - 28
                perm[i2, a * 32 + jj, col] = 1
    edge = np.zeros((2 * PAIRS * 16, ROWS * CELLS), np.float32)
    for side in range(2):
        for q in range(PAIRS):
            for r2 in range(2):
                for j in range(4):
                    cell = (CELLS - 4 + j) if side == 0 else j
                    edge[(side * PAIRS + q) * 16 + r2 * 4 + j, (q * 2 + r2) * CELLS + cell] = 1
    return [x.astype(jnp.bfloat16) for x in (sel_f, sel_b, perm, edge)]


def dot(a, b, dims=((1,), (0,))):
    return lax.dot_general(a, b, (dims, ((), ())), preferred_element_type=F32)


def kernel(
    lw, fields, cot, disco, up, down, filt, sel_f, sel_b, perm, edge,
    out_o, out_b, out_g,
    x, y, stage, vcot, vdisco, vup, vdown, vfilt, vself, vselb, vperm, vedge,
    vline, lines, band, tap_f, tap_b, spread, pre, cd, hidden, bpre, resid, bres, vout, vback,
    g, rc, a1, r1, a2, r2, rz, o,
    lsem, osem, hs, hr, cs, cr, s1s, s1r, s2s, s2r, zs, zr, g2s, g2r, g1s, g1r, gcs, gcr,
):
    lat, lon = lax.axis_index("lat"), lax.axis_index("lon")
    x_hi, yy = lat // 4, lat % 4
    zz, x_lo, core = lon // 4, (lon // 2) % 2, lon % 2
    xx = x_hi * 2 + x_lo

    def at_x(d):
        v = (xx + d) % 4
        return ((v // 2) * 4 + yy, zz * 4 + (v % 2) * 2 + core)

    def at_y(d):
        return (x_hi * 4 + (yy + d) % 4, lon)

    def at_z(d):
        return (lat, ((zz + d) % 8) * 4 + x_lo * 2 + core)

    pair = (lat, zz * 4 + x_lo * 2 + (1 - core))
    right, left = (lon + 1) % 32, (lon + 31) % 32
    has_up, has_down = lat > 0, lat < 7

    loads = [
        pltpu.make_async_copy(fields, x.at[:, 1:5, 0:48], lsem.at[0]),
        pltpu.make_async_copy(edge, vedge, lsem.at[1]),
        pltpu.make_async_copy(filt, vfilt, lsem.at[2]),
        pltpu.make_async_copy(sel_f, vself, lsem.at[3]),
        pltpu.make_async_copy(perm, vperm, lsem.at[4]),
        pltpu.make_async_copy(cot, vcot, lsem.at[5]),
        pltpu.make_async_copy(down, vdown, lsem.at[6]),
        pltpu.make_async_copy(disco, vdisco, lsem.at[7]),
        pltpu.make_async_copy(up, vup, lsem.at[8]),
        pltpu.make_async_copy(sel_b, vselb, lsem.at[9]),
    ]
    for c in loads:
        c.start()

    barrier = pltpu.get_barrier_semaphore()

    def hello(dev):
        pl.semaphore_signal(barrier, inc=1, device_id=dev, device_id_type=MESH)

    hello((lat, right))
    hello((lat, left))

    @pl.when(has_up)
    def _():
        for v in (left, lon, right):
            hello((lat - 1, v))

    @pl.when(has_down)
    def _():
        for v in (left, lon, right):
            hello((lat + 1, v))

    hello(pair)
    for d in range(1, 4):
        hello(at_x(d))
        hello(at_y(d))
    for d in range(1, 8):
        hello(at_z(d))

    zero48 = jnp.zeros((M, BLOCK, C), BF16)

    @pl.when(lat == 0)
    def _():
        x[:, 0] = zero48
        y[:, 0] = zero48

    @pl.when(lat == 7)
    def _():
        x[:, 5] = zero48
        y[:, 5] = zero48

    def rdma(src, dst, ss, rs, dev):
        return pltpu.make_async_remote_copy(
            src_ref=src, dst_ref=dst, send_sem=ss, recv_sem=rs, device_id=dev, device_id_type=MESH
        )

    def halo(buf, ph):
        st = stage.at[ph]

        def lon_copies():
            return [
                rdma(st.at[0], buf.at[:, 1:5, 48:64], hs.at[ph, 0], hr.at[ph, 0], (lat, right)),
                rdma(st.at[1], buf.at[:, 1:5, 64:80], hs.at[ph, 1], hr.at[ph, 1], (lat, left)),
            ]

        def to_down():
            return [
                rdma(buf.at[:, 4, 0:48], buf.at[:, 0, 0:48], hs.at[ph, 2], hr.at[ph, 2], (lat + 1, lon)),
                rdma(st.at[0, :, 3], buf.at[:, 0, 48:64], hs.at[ph, 3], hr.at[ph, 3], (lat + 1, right)),
                rdma(st.at[1, :, 3], buf.at[:, 0, 64:80], hs.at[ph, 4], hr.at[ph, 4], (lat + 1, left)),
            ]

        def to_up():
            return [
                rdma(buf.at[:, 1, 0:48], buf.at[:, 5, 0:48], hs.at[ph, 5], hr.at[ph, 5], (lat - 1, lon)),
                rdma(st.at[0, :, 0], buf.at[:, 5, 48:64], hs.at[ph, 6], hr.at[ph, 6], (lat - 1, right)),
                rdma(st.at[1, :, 0], buf.at[:, 5, 64:80], hs.at[ph, 7], hr.at[ph, 7], (lat - 1, left)),
            ]

        def start():
            @pl.when(has_down)
            def _():
                for c in to_down():
                    c.start()

            @pl.when(has_up)
            def _():
                for c in to_up():
                    c.start()

            for c in lon_copies():
                c.start()

        def recv():
            for c in lon_copies():
                c.wait_recv()

            @pl.when(has_up)
            def _():
                for c in to_down():
                    c.wait_recv()

            @pl.when(has_down)
            def _():
                for c in to_up():
                    c.wait_recv()

        def sent():
            for c in lon_copies():
                c.wait_send()

            @pl.when(has_down)
            def _():
                for c in to_down():
                    c.wait_send()

            @pl.when(has_up)
            def _():
                for c in to_up():
                    c.wait_send()

        return start, recv, sent

    halo_x = halo(x, 0)
    halo_y = halo(y, 1)

    def own(buf, m):
        return buf[m, 1:5, 0:48].reshape(ROWS * CELLS, C)

    def fill_stage(buf, ph):
        for m in range(M):
            e = dot(vedge[...], own(buf, m)).astype(BF16).reshape(2, PAIRS, 16, C)
            stage[ph, 0, m] = e[0]
            stage[ph, 1, m] = e[1]

    loads[0].wait()
    loads[1].wait()
    fill_stage(x, 0)
    pl.semaphore_wait(
        barrier, 16 + 3 * has_up.astype(jnp.int32) + 3 * has_down.astype(jnp.int32)
    )
    halo_x[0]()

    loads[2].wait()
    first = lat * ROWS - 2
    row_sel = (
        lax.broadcasted_iota(jnp.int32, (16, NLAT), 1)
        == lax.broadcasted_iota(jnp.int32, (16, NLAT), 0) + first
    )
    near = dot(jnp.where(row_sel, 1.0, 0.0).astype(BF16), vfilt[...]).astype(BF16)
    line_row = lax.broadcasted_iota(jnp.int32, (16, K * 256), 0)
    reach = jnp.zeros((16, K * 256), jnp.int32)
    for r in range(12):
        reach = jnp.where(line_row == r, lw[jnp.clip(first + r, 0, NLAT - 1)], reach)
    lane = lax.broadcasted_iota(jnp.int32, (16, K * 256), 1)
    keep = jnp.abs((lane & 31) - 4) <= reach

    def bands(get_line, tap):
        for i in range(ROWS):
            q, i2 = divmod(i, 2)
            parts = []
            for k in range(K):
                line = jnp.broadcast_to(get_line(i, k), (CELLS, 256))
                parts.append(
                    jnp.concatenate(
                        [
                            pltpu.roll(line[:, h * 128 : (h + 1) * 128], 0, 1, stride=1, stride_axis=0)
                            for h in range(2)
                        ],
                        axis=1,
                    )
                )
            band[i2, q * 96 : (q + 1) * 96] = jnp.concatenate(parts, axis=0).astype(BF16)
        res = [dot(band[i2], vperm[i2]) for i2 in range(2)]
        for q in range(PAIRS):
            for k in range(K):
                at = q * 96 + k * CELLS
                both = jnp.concatenate([res[0][at : at + CELLS], res[1][at : at + CELLS]], axis=0)
                tap[q, k * 48 : (k + 1) * 48] = both.astype(BF16)

    loads[3].wait()
    loads[4].wait()
    vline[...] = jnp.where(keep, dot(near, vself[...]), 0.0)
    bands(lambda i, k: vline[i + 2 : i + 3, k * 256 : (k + 1) * 256], tap_f)

    loads[5].wait()
    loads[6].wait()
    cd[...] = dot(vcot[...], vdown[...], ((1,), (1,)))
    loads[7].wait()
    loads[8].wait()
    loads[9].wait()

    def stencil(tap, buf, dst):
        for q in range(PAIRS):
            for m in range(M):
                res = dot(tap[q][:, :NK], buf[m, q : q + 3].reshape(NK, C)).astype(BF16)
                for k in range(K):
                    at = m * 192 + q * 48
                    dst[at : at + 48, k * C : (k + 1) * C] = res[k * 48 : (k + 1) * 48]

    halo_x[1]()
    stencil(tap_f, x, spread)

    for m in range(M):
        mixed = dot(spread[m * 192 : (m + 1) * 192], vdisco[...])
        resid[m * 192 : (m + 1) * 192] = (own(x, m).astype(F32) + mixed).astype(BF16)
    pre[...] = dot(resid[...], vup[...])

    @pl.loop(0, TOK // 16)
    def _(n):
        at = pl.ds(pl.multiple_of(n * 16, 16), 16)
        p = pre[at]
        pp = p * p
        t = jnp.tanh(GELU_SCALE * p * (1.0 + GELU_CUBE * pp))
        h = 0.5 * (1.0 + t)
        hidden[at] = (p * h).astype(BF16)
        slope = h + 0.5 * p * (1.0 - t * t) * GELU_SCALE * (1.0 + 3.0 * GELU_CUBE * pp)
        bpre[at] = (cd[at] * slope).astype(BF16)

    rows0 = ((0,), (0,))

    def put(n, value):
        g[n] = value.astype(BF16).reshape(2, 4, 4, 16, C)

    def core_copy(n):
        return rdma(g.at[n, 1 - core], rc.at[n], cs.at[n], cr.at[n], pair)

    put(0, dot(hidden[...], vcot[...], rows0))
    core_copy(0).start()
    gu = dot(resid[...], bpre[...], rows0)
    put(1, jnp.concatenate([gu[:, :C], gu[:, C:]], axis=0))
    core_copy(1).start()

    br = (vcot[...].astype(F32) + dot(bpre[...], vup[...], ((1,), (1,)))).astype(BF16)
    bres[...] = br
    for m in range(M):
        y[m, 1:5, 0:48] = br[m * 192 : (m + 1) * 192].reshape(PAIRS, 48, C)
    fill_stage(y, 1)
    halo_y[0]()
    for n in range(2):
        put(2 + n, dot(spread[:, n * 512 : (n + 1) * 512], bres[...], rows0))
        core_copy(2 + n).start()

    def ways(n):
        return ((at_x, xx), (at_y, yy)) if n % 2 == 0 else ((at_y, yy), (at_x, xx))

    def s1_copies(n):
        peer, me = ways(n)[0]
        return [
            rdma(a1.at[n, (me + d) % 4], r1.at[n, d - 1], s1s.at[n, d - 1], s1r.at[n, d - 1], peer(d))
            for d in range(1, 4)
        ]

    def s2_copies(n):
        peer, me = ways(n)[1]
        return [
            rdma(a2.at[n, (me + d) % 4], r2.at[n, d - 1], s2s.at[n, d - 1], s2r.at[n, d - 1], peer(d))
            for d in range(1, 4)
        ]

    def z_copies(h):
        return [
            rdma(rz.at[h, zz], rz.at[h, zz], zs.at[h, d - 1], zr.at[h, d - 1], at_z(d))
            for d in range(1, 8)
        ]

    def g2_copies(n):
        (_, m1), (peer, m2) = ways(n)
        ref = o.at[n, core, m1, m2]
        return [rdma(ref, ref, g2s.at[n, d - 1], g2r.at[n, d - 1], peer(d)) for d in range(1, 4)]

    def g1_copies(n):
        peer, m1 = ways(n)[0]
        ref = o.at[n, core, m1]
        return [rdma(ref, ref, g1s.at[n, d - 1], g1r.at[n, d - 1], peer(d)) for d in range(1, 4)]

    def gc_copy(n):
        ref = o.at[n, core]
        return rdma(ref, ref, gcs.at[n], gcr.at[n], pair)

    def start(cs_):
        for c in cs_:
            c.start()

    def recv(cs_):
        for c in cs_:
            c.wait_recv()

    def do_core(n):
        core_copy(n).wait_recv()
        a1[n] = (g[n, core].astype(F32) + rc[n].astype(F32)).astype(BF16)
        start(s1_copies(n))

    def do_s1(n):
        recv(s1_copies(n))
        me = ways(n)[0][1]
        v = a1[n, me].astype(F32)
        for d in range(3):
            v = v + r1[n, d].astype(F32)
        a2[n] = v.astype(BF16)
        start(s2_copies(n))

    def do_s2(h):
        for e in range(2):
            n = 2 * h + e
            recv(s2_copies(n))
            me = ways(n)[1][1]
            v = a2[n, me].astype(F32)
            for d in range(3):
                v = v + r2[n, d].astype(F32)
            rz[h, zz, e] = v.astype(BF16)
        start(z_copies(h))

    def do_z(h):
        recv(z_copies(h))
        v = rz[h, 0].astype(F32)
        for d in range(1, 8):
            v = v + rz[h, d].astype(F32)
        v = v.astype(BF16)
        for e in range(2):
            n = 2 * h + e
            (_, m1), (_, m2) = ways(n)
            o[n, core, m1, m2] = v[e]
            start(g2_copies(n))

    def do_g2(n):
        recv(g2_copies(n))
        start(g1_copies(n))

    def do_g1(n):
        recv(g1_copies(n))
        gc_copy(n).start()

    do_core(0)
    do_core(1)
    do_core(2)
    do_core(3)

    vline[...] = jnp.where(keep, dot(near, vselb[...]), 0.0)
    group = (lax.broadcasted_iota(jnp.int32, (8, K * 256), 1) // 32) % 8
    total = jnp.zeros((8, K * 256), F32)
    for r in range(A_TAPS):
        total = total + jnp.where(group == r, vline[r : r + 8], 0.0)
    lines[...] = total
    bands(lambda i, k: lines[i : i + 1, k * 256 : (k + 1) * 256], tap_b)

    for n in range(4):
        do_s1(n)
    vout[...] = (resid[...].astype(F32) + dot(hidden[...], vdown[...])).astype(BF16)
    put_o = pltpu.make_async_copy(vout, out_o, osem.at[0])
    put_o.start()
    do_s2(0)
    do_s2(1)

    halo_y[1]()
    stencil(tap_b, y, spread)
    do_z(0)
    do_z(1)
    for m in range(M):
        at = slice(m * 192, (m + 1) * 192)
        acc = bres[at].astype(F32)
        for k in range(K):
            acc = acc + dot(
                spread[at, k * C : (k + 1) * C], vdisco[k * C : (k + 1) * C], ((1,), (1,))
            )
        vback[at] = acc.astype(BF16)
    put_b = pltpu.make_async_copy(vback, out_b, osem.at[1])
    put_b.start()
    for n in range(4):
        do_g2(n)
    for n in range(4):
        do_g1(n)
    for n in range(4):
        gc_copy(n).wait_recv()
    put_g = pltpu.make_async_copy(o, out_g, osem.at[2])
    put_g.start()

    halo_x[2]()
    halo_y[2]()
    for n in range(4):
        core_copy(n).wait_send()
        for c in s1_copies(n) + s2_copies(n) + g2_copies(n) + g1_copies(n):
            c.wait_send()
        gc_copy(n).wait_send()
    for h in range(2):
        for c in z_copies(h):
            c.wait_send()
    put_o.wait()
    put_b.wait()
    put_g.wait()


def per_device(fields, filters, lon_width, disco_weight, up_weight, down_weight, cotangent):
    flat = jnp.pad(filters.reshape(NLAT, A_TAPS * B_TAPS * K), ((0, 0), (0, 76)))
    sel_f, sel_b, perm, edge = [jnp.asarray(v) for v in constants()]
    anyspec = pl.BlockSpec(memory_space=pl.ANY)
    dma = pltpu.SemaphoreType.DMA
    vm = pltpu.VMEM
    scratch = [
        vm((M, 6, BLOCK, C), BF16),
        vm((M, 6, BLOCK, C), BF16),
        vm((2, 2, M, PAIRS, 16, C), BF16),
        vm((TOK, C), BF16),
        vm((K * C, C), BF16),
        vm((C, FF), BF16),
        vm((FF, C), BF16),
        vm((NLAT, 256), BF16),
        vm((256, K * 256), BF16),
        vm((256, K * 256), BF16),
        vm((2, 256, 256), BF16),
        vm((2 * PAIRS * 16, ROWS * CELLS), BF16),
        vm((16, K * 256), F32),
        vm((8, K * 256), F32),
        vm((2, PAIRS * 96, 256), BF16),
        vm((PAIRS, 192, 256), BF16),
        vm((PAIRS, 192, 256), BF16),
        vm((TOK, K * C), BF16),
        vm((TOK, FF), F32),
        vm((TOK, FF), F32),
        vm((TOK, FF), BF16),
        vm((TOK, FF), BF16),
        vm((TOK, C), BF16),
        vm((TOK, C), BF16),
        vm((TOK, C), BF16),
        vm((TOK, C), BF16),
        vm((4, 2, 4, 4, 16, C), BF16),
        vm((4, 4, 4, 16, C), BF16),
        vm((4, 4, 4, 16, C), BF16),
        vm((4, 3, 4, 16, C), BF16),
        vm((4, 4, 16, C), BF16),
        vm((4, 3, 16, C), BF16),
        vm((2, 8, 2, 16, C), BF16),
        vm((4, 2, 4, 4, 16, C), BF16),
        dma((10,)),
        dma((3,)),
        dma((2, 8)),
        dma((2, 8)),
        dma((4,)),
        dma((4,)),
        dma((4, 3)),
        dma((4, 3)),
        dma((4, 3)),
        dma((4, 3)),
        dma((2, 7)),
        dma((2, 7)),
        dma((4, 3)),
        dma((4, 3)),
        dma((4, 3)),
        dma((4, 3)),
        dma((4,)),
        dma((4,)),
    ]
    out_o, out_b, out_g = pl.pallas_call(
        kernel,
        out_shape=(
            jax.ShapeDtypeStruct((TOK, C), BF16),
            jax.ShapeDtypeStruct((TOK, C), BF16),
            jax.ShapeDtypeStruct((4, 2, 4, 4, 16, C), BF16),
        ),
        in_specs=[pl.BlockSpec(memory_space=pltpu.SMEM)] + [anyspec] * 10,
        out_specs=(anyspec, anyspec, anyspec),
        scratch_shapes=scratch,
        compiler_params=pltpu.CompilerParams(
            collective_id=0, has_side_effects=True, vmem_limit_bytes=40 * 2**20
        ),
    )(
        lon_width,
        fields.reshape(M, PAIRS, 48, C),
        cotangent.reshape(TOK, C),
        disco_weight.reshape(K * C, C),
        up_weight,
        down_weight,
        flat,
        sel_f,
        sel_b,
        perm,
        edge,
    )
    grads = out_g.reshape(4, 512, C).astype(F32)
    grad_up = jnp.concatenate([grads[1, :C], grads[1, C:]], axis=1)
    shape = fields.shape
    return (
        out_o.reshape(shape),
        out_b.reshape(shape),
        grads[2:].reshape(K, C, C),
        grad_up,
        grads[0],
    )


def solution(mesh):
    placed = (P(None, "lat", "lon", None), P(), P(), P(), P(), P(), P(None, "lat", "lon", None))
    return jax.shard_map(
        per_device,
        mesh=mesh,
        in_specs=placed,
        out_specs=(P(None, "lat", "lon", None), P(None, "lat", "lon", None), P(), P(), P()),
        check_vma=False,
    )
```

```python
import functools

import jax
import jax.numpy as jnp
import numpy as np
from jax import lax
from jax.experimental import pallas as pl
from jax.experimental.pallas import tpu as pltpu
from jax.sharding import PartitionSpec as P

GELU_SCALE = 0.7978845608028654
GELU_CUBE = 0.044715
MESH = pl.DeviceIdType.MESH
F32 = jnp.float32
BF16 = jnp.bfloat16

M, ROWS, CELLS, C, FF, K = 2, 8, 24, 256, 512, 4
NLAT = 64
A_TAPS, B_TAPS = 5, 9
PAIRS = ROWS // 2
TOK = M * ROWS * CELLS
BLOCK = 80
NK = 3 * BLOCK
NF = A_TAPS * B_TAPS * 8


def constants():
    sel_f = np.zeros((NF, K * 256), np.float32)
    sel_b = np.zeros((NF, K * 256), np.float32)
    for a in range(A_TAPS):
        for b in range(B_TAPS):
            for k in range(K):
                s = (a * B_TAPS + b) * 8 + k
                sel_f[s, k * 256 + a * 32 + b] = 1
                sel_b[s, k * 256 + (4 - a) * 32 + 8 - b] = 1
    perm = np.zeros((2, 256, 256), np.float32)
    for i2 in range(2):
        for a in range(A_TAPS):
            p, r2 = divmod(i2 + a, 2)
            for jj in range(32):
                if jj < 4:
                    col = p * BLOCK + 48 + r2 * 4 + jj
                elif jj < 28:
                    col = p * BLOCK + r2 * CELLS + jj - 4
                else:
                    col = p * BLOCK + 64 + r2 * 4 + jj - 28
                perm[i2, a * 32 + jj, col] = 1
    edge = np.zeros((2 * PAIRS * 16, ROWS * CELLS), np.float32)
    for side in range(2):
        for q in range(PAIRS):
            for r2 in range(2):
                for j in range(4):
                    cell = (CELLS - 4 + j) if side == 0 else j
                    edge[(side * PAIRS + q) * 16 + r2 * 4 + j, (q * 2 + r2) * CELLS + cell] = 1
    return [x.astype(jnp.bfloat16) for x in (sel_f, sel_b, perm, edge)]


def dot(a, b, dims=((1,), (0,))):
    return lax.dot_general(a, b, (dims, ((), ())), preferred_element_type=F32)


def kernel(
    lw, fields, cot, disco, up, down, filt, sel_f, sel_b, perm, edge,
    vout, vback, o,
    x, y, stage, vcot, vdisco, vup, vdown, vfilt, filt8, vself, vselb, vperm, vedge,
    vline, lines, band, tap_f, tap_b, spread, pre, cd, hidden, bpre, resid, bres,
    g, rc, a1, r1, a2, r2, rz,
    lsem, hs, hr, cs, cr, s1s, s1r, s2s, s2r, zs, zr, g2s, g2r, g1s, g1r, gcs, gcr,
):
    lat, lon = lax.axis_index("lat"), lax.axis_index("lon")
    x_hi, yy = lat // 4, lat % 4
    zz, x_lo, core = lon // 4, (lon // 2) % 2, lon % 2
    xx = x_hi * 2 + x_lo

    def at_x(d):
        v = (xx + d) % 4
        return ((v // 2) * 4 + yy, zz * 4 + (v % 2) * 2 + core)

    def at_y(d):
        return (x_hi * 4 + (yy + d) % 4, lon)

    def at_z(d):
        return (lat, ((zz + d) % 8) * 4 + x_lo * 2 + core)

    pair = (lat, zz * 4 + x_lo * 2 + (1 - core))
    right, left = (lon + 1) % 32, (lon + 31) % 32
    has_up, has_down = lat > 0, lat < 7

    loads = [
        pltpu.make_async_copy(fields, x.at[:, 1:5, 0:48], lsem.at[0]),
        pltpu.make_async_copy(edge, vedge, lsem.at[1]),
        pltpu.make_async_copy(filt, vfilt, lsem.at[2]),
        pltpu.make_async_copy(sel_f, vself, lsem.at[3]),
        pltpu.make_async_copy(perm, vperm, lsem.at[4]),
        pltpu.make_async_copy(cot, vcot, lsem.at[5]),
        pltpu.make_async_copy(down, vdown, lsem.at[6]),
        pltpu.make_async_copy(disco, vdisco, lsem.at[7]),
        pltpu.make_async_copy(up, vup, lsem.at[8]),
        pltpu.make_async_copy(sel_b, vselb, lsem.at[9]),
    ]
    for c in loads:
        c.start()

    barrier = pltpu.get_barrier_semaphore()

    def hello(dev):
        pl.semaphore_signal(barrier, inc=1, device_id=dev, device_id_type=MESH)

    hello((lat, right))
    hello((lat, left))

    @pl.when(has_up)
    def _():
        for v in (left, lon, right):
            hello((lat - 1, v))

    @pl.when(has_down)
    def _():
        for v in (left, lon, right):
            hello((lat + 1, v))

    hello(pair)
    for d in range(1, 4):
        hello(at_x(d))
        hello(at_y(d))
    for d in range(1, 8):
        hello(at_z(d))

    zero48 = jnp.zeros((M, BLOCK, C), BF16)

    @pl.when(lat == 0)
    def _():
        x[:, 0] = zero48
        y[:, 0] = zero48

    @pl.when(lat == 7)
    def _():
        x[:, 5] = zero48
        y[:, 5] = zero48

    def rdma(src, dst, ss, rs, dev):
        return pltpu.make_async_remote_copy(
            src_ref=src, dst_ref=dst, send_sem=ss, recv_sem=rs, device_id=dev, device_id_type=MESH
        )

    def halo(buf, ph):
        st = stage.at[ph]

        def lon_copies():
            return [
                rdma(st.at[0], buf.at[:, 1:5, 48:64], hs.at[ph, 0], hr.at[ph, 0], (lat, right)),
                rdma(st.at[1], buf.at[:, 1:5, 64:80], hs.at[ph, 1], hr.at[ph, 1], (lat, left)),
            ]

        def to_down():
            return [
                rdma(buf.at[:, 4, 0:48], buf.at[:, 0, 0:48], hs.at[ph, 2], hr.at[ph, 2], (lat + 1, lon)),
                rdma(st.at[0, :, 3], buf.at[:, 0, 48:64], hs.at[ph, 3], hr.at[ph, 3], (lat + 1, right)),
                rdma(st.at[1, :, 3], buf.at[:, 0, 64:80], hs.at[ph, 4], hr.at[ph, 4], (lat + 1, left)),
            ]

        def to_up():
            return [
                rdma(buf.at[:, 1, 0:48], buf.at[:, 5, 0:48], hs.at[ph, 5], hr.at[ph, 5], (lat - 1, lon)),
                rdma(st.at[0, :, 0], buf.at[:, 5, 48:64], hs.at[ph, 6], hr.at[ph, 6], (lat - 1, right)),
                rdma(st.at[1, :, 0], buf.at[:, 5, 64:80], hs.at[ph, 7], hr.at[ph, 7], (lat - 1, left)),
            ]

        def start():
            @pl.when(has_down)
            def _():
                for c in to_down():
                    c.start()

            @pl.when(has_up)
            def _():
                for c in to_up():
                    c.start()

            for c in lon_copies():
                c.start()

        def recv():
            for c in lon_copies():
                c.wait_recv()

            @pl.when(has_up)
            def _():
                for c in to_down():
                    c.wait_recv()

            @pl.when(has_down)
            def _():
                for c in to_up():
                    c.wait_recv()

        def sent():
            for c in lon_copies():
                c.wait_send()

            @pl.when(has_down)
            def _():
                for c in to_down():
                    c.wait_send()

            @pl.when(has_up)
            def _():
                for c in to_up():
                    c.wait_send()

        return start, recv, sent

    halo_x = halo(x, 0)
    halo_y = halo(y, 1)

    def own(buf, m):
        return buf[m, 1:5, 0:48].reshape(ROWS * CELLS, C)

    def fill_stage(buf, ph):
        for m in range(M):
            e = dot(vedge[...], own(buf, m)).astype(BF16).reshape(2, PAIRS, 16, C)
            stage[ph, 0, m] = e[0]
            stage[ph, 1, m] = e[1]

    loads[0].wait()
    loads[1].wait()
    fill_stage(x, 0)
    pl.semaphore_wait(
        barrier, 16 + 3 * has_up.astype(jnp.int32) + 3 * has_down.astype(jnp.int32)
    )
    halo_x[0]()

    loads[2].wait()
    filt8[...] = jnp.zeros_like(filt8)
    for n in range(A_TAPS * B_TAPS):
        filt8[n * 8 : n * 8 + K] = vfilt[n].astype(F32)
    first = lat * ROWS - 2
    row_sel = (
        lax.broadcasted_iota(jnp.int32, (16, NLAT), 1)
        == lax.broadcasted_iota(jnp.int32, (16, NLAT), 0) + first
    )
    near = dot(jnp.where(row_sel, 1.0, 0.0).astype(BF16), filt8[...].astype(BF16), ((1,), (1,))).astype(BF16)
    line_row = lax.broadcasted_iota(jnp.int32, (16, K * 256), 0)
    reach = jnp.zeros((16, K * 256), jnp.int32)
    for r in range(12):
        reach = jnp.where(line_row == r, lw[jnp.clip(first + r, 0, NLAT - 1)], reach)
    lane = lax.broadcasted_iota(jnp.int32, (16, K * 256), 1)
    keep = jnp.abs((lane & 31) - 4) <= reach

    def bands(get_line, tap):
        for i in range(ROWS):
            q, i2 = divmod(i, 2)
            parts = []
            for k in range(K):
                line = jnp.broadcast_to(get_line(i, k), (CELLS, 256))
                parts.append(
                    jnp.concatenate(
                        [
                            pltpu.roll(line[:, h * 128 : (h + 1) * 128], 0, 1, stride=1, stride_axis=0)
                            for h in range(2)
                        ],
                        axis=1,
                    )
                )
            band[i2, q * 96 : (q + 1) * 96] = jnp.concatenate(parts, axis=0).astype(BF16)
        res = [dot(band[i2], vperm[i2]) for i2 in range(2)]
        for q in range(PAIRS):
            for k in range(K):
                at = q * 96 + k * CELLS
                both = jnp.concatenate([res[0][at : at + CELLS], res[1][at : at + CELLS]], axis=0)
                tap[q, k * 48 : (k + 1) * 48] = both.astype(BF16)

    loads[3].wait()
    loads[4].wait()
    vline[...] = jnp.where(keep, dot(near, vself[...]), 0.0)
    bands(lambda i, k: vline[i + 2 : i + 3, k * 256 : (k + 1) * 256], tap_f)

    loads[5].wait()
    loads[6].wait()
    cd[...] = dot(vcot[...], vdown[...], ((1,), (1,)))
    loads[9].wait()
    vline[...] = jnp.where(keep, dot(near, vselb[...]), 0.0)
    group = (lax.broadcasted_iota(jnp.int32, (8, K * 256), 1) // 32) % 8
    total = jnp.zeros((8, K * 256), F32)
    for r in range(A_TAPS):
        total = total + jnp.where(group == r, vline[r : r + 8], 0.0)
    lines[...] = total
    bands(lambda i, k: lines[i : i + 1, k * 256 : (k + 1) * 256], tap_b)

    loads[7].wait()
    loads[8].wait()

    def stencil(tap, buf, dst):
        for q in range(PAIRS):
            for m in range(M):
                res = dot(tap[q][:, :NK], buf[m, q : q + 3].reshape(NK, C)).astype(BF16)
                for k in range(K):
                    at = m * 192 + q * 48
                    dst[at : at + 48, k * C : (k + 1) * C] = res[k * 48 : (k + 1) * 48]

    halo_x[1]()
    stencil(tap_f, x, spread)

    for m in range(M):
        mixed = dot(spread[m * 192 : (m + 1) * 192], vdisco[...])
        resid[m * 192 : (m + 1) * 192] = (own(x, m).astype(F32) + mixed).astype(BF16)
    pre[...] = dot(resid[...], vup[...])

    @pl.loop(0, TOK // 16)
    def _(n):
        at = pl.ds(pl.multiple_of(n * 16, 16), 16)
        p = pre[at]
        pp = p * p
        t = jnp.tanh(GELU_SCALE * p * (1.0 + GELU_CUBE * pp))
        h = 0.5 * (1.0 + t)
        hidden[at] = (p * h).astype(BF16)
        slope = h + 0.5 * p * (1.0 - t * t) * GELU_SCALE * (1.0 + 3.0 * GELU_CUBE * pp)
        bpre[at] = (cd[at] * slope).astype(BF16)

    rows0 = ((0,), (0,))

    def put(n, value):
        g[n] = value.astype(BF16).reshape(2, 4, 4, 16, C)

    def core_copy(n):
        return rdma(g.at[n, 1 - core], rc.at[n], cs.at[n], cr.at[n], pair)

    put(0, dot(hidden[...], vcot[...], rows0))
    core_copy(0).start()
    gu = dot(resid[...], bpre[...], rows0)
    put(1, jnp.concatenate([gu[:, :C], gu[:, C:]], axis=0))
    core_copy(1).start()

    def ways(n):
        return ((at_x, xx), (at_y, yy)) if n % 2 == 0 else ((at_y, yy), (at_x, xx))

    def s1_copies(n):
        peer, me = ways(n)[0]
        return [
            rdma(a1.at[n, (me + d) % 4], r1.at[n, d - 1], s1s.at[n, d - 1], s1r.at[n, d - 1], peer(d))
            for d in range(1, 4)
        ]

    def s2_copies(n):
        peer, me = ways(n)[1]
        return [
            rdma(a2.at[n, (me + d) % 4], r2.at[n, d - 1], s2s.at[n, d - 1], s2r.at[n, d - 1], peer(d))
            for d in range(1, 4)
        ]

    def z_copies(h):
        return [
            rdma(rz.at[h, zz], rz.at[h, zz], zs.at[h, d - 1], zr.at[h, d - 1], at_z(d))
            for d in range(1, 8)
        ]

    def g2_copies(n):
        (_, m1), (peer, m2) = ways(n)
        ref = o.at[n, core, m1, m2]
        return [rdma(ref, ref, g2s.at[n, d - 1], g2r.at[n, d - 1], peer(d)) for d in range(1, 4)]

    def g1_copies(n):
        peer, m1 = ways(n)[0]
        ref = o.at[n, core, m1]
        return [rdma(ref, ref, g1s.at[n, d - 1], g1r.at[n, d - 1], peer(d)) for d in range(1, 4)]

    def gc_copy(n):
        ref = o.at[n, core]
        return rdma(ref, ref, gcs.at[n], gcr.at[n], pair)

    def start(cs_):
        for c in cs_:
            c.start()

    def recv(cs_):
        for c in cs_:
            c.wait_recv()

    def do_core(n):
        core_copy(n).wait_recv()
        a1[n] = (g[n, core].astype(F32) + rc[n].astype(F32)).astype(BF16)
        start(s1_copies(n))

    def do_s1(n):
        recv(s1_copies(n))
        me = ways(n)[0][1]
        v = a1[n, me].astype(F32)
        for d in range(3):
            v = v + r1[n, d].astype(F32)
        a2[n] = v.astype(BF16)
        start(s2_copies(n))

    def do_s2(h):
        for e in range(2):
            n = 2 * h + e
            recv(s2_copies(n))
            me = ways(n)[1][1]
            v = a2[n, me].astype(F32)
            for d in range(3):
                v = v + r2[n, d].astype(F32)
            rz[h, zz, e] = v.astype(BF16)
        start(z_copies(h))

    def do_z(h):
        recv(z_copies(h))
        v = rz[h, 0].astype(F32)
        for d in range(1, 8):
            v = v + rz[h, d].astype(F32)
        v = v.astype(BF16)
        for e in range(2):
            n = 2 * h + e
            (_, m1), (_, m2) = ways(n)
            o[n, core, m1, m2] = v[e]
            start(g2_copies(n))

    def do_g2(n):
        recv(g2_copies(n))
        start(g1_copies(n))

    def do_g1(n):
        recv(g1_copies(n))
        gc_copy(n).start()

    br = (vcot[...].astype(F32) + dot(bpre[...], vup[...], ((1,), (1,)))).astype(BF16)
    bres[...] = br
    for m in range(M):
        y[m, 1:5, 0:48] = br[m * 192 : (m + 1) * 192].reshape(PAIRS, 48, C)
    fill_stage(y, 1)
    do_core(0)
    do_core(1)
    for n in range(2):
        put(2 + n, dot(spread[:, n * 512 : (n + 1) * 512], bres[...], rows0))
        core_copy(2 + n).start()

    do_core(2)
    do_core(3)
    for n in range(4):
        do_s1(n)
    do_s2(0)
    do_s2(1)

    halo_y[0]()
    vout[...] = (resid[...].astype(F32) + dot(hidden[...], vdown[...])).astype(BF16)
    do_z(0)
    do_z(1)
    halo_y[1]()
    stencil(tap_b, y, spread)
    for m in range(M):
        at = slice(m * 192, (m + 1) * 192)
        acc = bres[at].astype(F32)
        for k in range(K):
            acc = acc + dot(
                spread[at, k * C : (k + 1) * C], vdisco[k * C : (k + 1) * C], ((1,), (1,))
            )
        vback[at] = acc.astype(BF16)

    for n in range(4):
        do_g2(n)
    for n in range(4):
        do_g1(n)

    for n in range(4):
        gc_copy(n).wait_recv()

    halo_x[2]()
    halo_y[2]()
    for n in range(4):
        core_copy(n).wait_send()
        for c in s1_copies(n) + s2_copies(n) + g2_copies(n) + g1_copies(n):
            c.wait_send()
        gc_copy(n).wait_send()
    for h in range(2):
        for c in z_copies(h):
            c.wait_send()


def finish(o, b, g, out_o, out_b, out_disco, out_up, out_down, wdisco, wup, wdown, sem):
    copies = [
        pltpu.make_async_copy(o, out_o, sem.at[0]),
        pltpu.make_async_copy(b, out_b, sem.at[1]),
        pltpu.make_async_copy(wdisco, out_disco, sem.at[2]),
        pltpu.make_async_copy(wdown, out_down, sem.at[3]),
        pltpu.make_async_copy(wup, out_up, sem.at[4]),
    ]
    copies[0].start()
    copies[1].start()
    wdisco[...] = g[2:].reshape(K * C, C).astype(F32)
    copies[2].start()
    wdown[...] = g[0].reshape(FF, C).astype(F32)
    copies[3].start()
    wup[:, :C] = g[1, 0].reshape(C, C).astype(F32)
    wup[:, C:] = g[1, 1].reshape(C, C).astype(F32)
    copies[4].start()
    for c in copies:
        c.wait()


def per_device(fields, filters, lon_width, disco_weight, up_weight, down_weight, cotangent):
    flat = filters.transpose(1, 2, 3, 0).reshape(A_TAPS * B_TAPS, K, NLAT)
    sel_f, sel_b, perm, edge = [jnp.asarray(v) for v in constants()]
    vspec = pl.BlockSpec(memory_space=pltpu.VMEM)
    anyspec = pl.BlockSpec(memory_space=pl.ANY)
    dma = pltpu.SemaphoreType.DMA
    vm = pltpu.VMEM
    scratch = [
        vm((M, 6, BLOCK, C), BF16),
        vm((M, 6, BLOCK, C), BF16),
        vm((2, 2, M, PAIRS, 16, C), BF16),
        vm((TOK, C), BF16),
        vm((K * C, C), BF16),
        vm((C, FF), BF16),
        vm((FF, C), BF16),
        vm((A_TAPS * B_TAPS, K, NLAT), BF16),
        vm((NF, NLAT), F32),
        vm((NF, K * 256), BF16),
        vm((NF, K * 256), BF16),
        vm((2, 256, 256), BF16),
        vm((2 * PAIRS * 16, ROWS * CELLS), BF16),
        vm((16, K * 256), F32),
        vm((8, K * 256), F32),
        vm((2, PAIRS * 96, 256), BF16),
        vm((PAIRS, 192, 256), BF16),
        vm((PAIRS, 192, 256), BF16),
        vm((TOK, K * C), BF16),
        vm((TOK, FF), F32),
        vm((TOK, FF), F32),
        vm((TOK, FF), BF16),
        vm((TOK, FF), BF16),
        vm((TOK, C), BF16),
        vm((TOK, C), BF16),
        vm((4, 2, 4, 4, 16, C), BF16),
        vm((4, 4, 4, 16, C), BF16),
        vm((4, 4, 4, 16, C), BF16),
        vm((4, 3, 4, 16, C), BF16),
        vm((4, 4, 16, C), BF16),
        vm((4, 3, 16, C), BF16),
        vm((2, 8, 2, 16, C), BF16),
        dma((10,)),
        dma((2, 8)),
        dma((2, 8)),
        dma((4,)),
        dma((4,)),
        dma((4, 3)),
        dma((4, 3)),
        dma((4, 3)),
        dma((4, 3)),
        dma((2, 7)),
        dma((2, 7)),
        dma((4, 3)),
        dma((4, 3)),
        dma((4, 3)),
        dma((4, 3)),
        dma((4,)),
        dma((4,)),
    ]
    inner = pl.pallas_call(
        kernel,
        out_shape=(
            vm((TOK, C), BF16),
            vm((TOK, C), BF16),
            vm((4, 2, 4, 4, 16, C), BF16),
        ),
        in_specs=[pl.BlockSpec(memory_space=pltpu.SMEM)] + [pl.BlockSpec(memory_space=pltpu.HBM)] * 10,
        out_specs=[vspec] * 3,
        scratch_shapes=scratch,
        compiler_params=pltpu.CompilerParams(
            collective_id=0, has_side_effects=True, vmem_limit_bytes=62 * 2**20
        ),
    )(
        lon_width,
        fields.reshape(M, PAIRS, 48, C),
        cotangent.reshape(TOK, C),
        disco_weight.reshape(K * C, C),
        up_weight,
        down_weight,
        flat,
        sel_f,
        sel_b,
        perm,
        edge,
    )
    out, back, disco, up, down = pl.pallas_call(
        finish,
        out_shape=(
            jax.ShapeDtypeStruct((TOK, C), BF16),
            jax.ShapeDtypeStruct((TOK, C), BF16),
            jax.ShapeDtypeStruct((K * C, C), F32),
            jax.ShapeDtypeStruct((C, FF), F32),
            jax.ShapeDtypeStruct((FF, C), F32),
        ),
        in_specs=[vspec] * 3,
        out_specs=[pl.BlockSpec(memory_space=pltpu.HBM)] * 5,
        scratch_shapes=[vm((K * C, C), F32), vm((C, FF), F32), vm((FF, C), F32), dma((5,))],
        compiler_params=pltpu.CompilerParams(vmem_limit_bytes=16 * 2**20),
    )(*[pltpu.with_memory_space_constraint(v, pltpu.VMEM) for v in inner])
    shape = fields.shape
    return out.reshape(shape), back.reshape(shape), disco.reshape(K, C, C), up, down


def solution(mesh):
    placed = (P(None, "lat", "lon", None), P(), P(), P(), P(), P(), P(None, "lat", "lon", None))
    return jax.shard_map(
        per_device,
        mesh=mesh,
        in_specs=placed,
        out_specs=(P(None, "lat", "lon", None), P(None, "lat", "lon", None), P(), P(), P()),
        check_vma=False,
    )
```

```python
import functools

import jax
import jax.numpy as jnp
import numpy as np
from jax import lax
from jax.experimental import pallas as pl
from jax.experimental.pallas import tpu as pltpu
from jax.sharding import PartitionSpec as P

GELU_SCALE = 0.7978845608028654
GELU_CUBE = 0.044715
MESH = pl.DeviceIdType.MESH
F32 = jnp.float32
BF16 = jnp.bfloat16

M, ROWS, CELLS, C, FF, K = 2, 8, 24, 256, 512, 4
NLAT = 64
A_TAPS, B_TAPS = 5, 9
PAIRS = ROWS // 2
TOK = M * ROWS * CELLS
BLOCK = 80
NK = 3 * BLOCK
NF = A_TAPS * B_TAPS * 8
PLANE = sorted(
    [(dx, dy) for dx in range(4) for dy in range(4) if dx or dy],
    key=lambda t: (-min(t[0], 4 - t[0]) - min(t[1], 4 - t[1]), t),
)
RING = (4, 3, 5, 2, 6, 1, 7)


def constants():
    sel_f = np.zeros((NF, K * 256), np.float32)
    sel_b = np.zeros((NF, K * 256), np.float32)
    for a in range(A_TAPS):
        for b in range(B_TAPS):
            for k in range(K):
                s = (a * B_TAPS + b) * 8 + k
                sel_f[s, k * 256 + a * 32 + b] = 1
                sel_b[s, k * 256 + (4 - a) * 32 + 8 - b] = 1
    perm = np.zeros((2, 256, 256), np.float32)
    for i2 in range(2):
        for a in range(A_TAPS):
            p, r2 = divmod(i2 + a, 2)
            for jj in range(32):
                if jj < 4:
                    col = p * BLOCK + 48 + r2 * 4 + jj
                elif jj < 28:
                    col = p * BLOCK + r2 * CELLS + jj - 4
                else:
                    col = p * BLOCK + 64 + r2 * 4 + jj - 28
                perm[i2, a * 32 + jj, col] = 1
    edge = np.zeros((2 * PAIRS * 16, ROWS * CELLS), np.float32)
    for side in range(2):
        for q in range(PAIRS):
            for r2 in range(2):
                for j in range(4):
                    cell = (CELLS - 4 + j) if side == 0 else j
                    edge[(side * PAIRS + q) * 16 + r2 * 4 + j, (q * 2 + r2) * CELLS + cell] = 1
    return [x.astype(jnp.bfloat16) for x in (sel_f, sel_b, perm, edge)]


def dot(a, b, dims=((1,), (0,))):
    return lax.dot_general(a, b, (dims, ((), ())), preferred_element_type=F32)


def kernel(
    lw, fields, cot, disco, up, down, filt, sel_f, sel_b, perm, edge,
    vout, vback, o,
    x, y, stage, vcot, vdisco, vup, vdown, vfilt, filt8, vself, vselb, vperm, vedge,
    vline, lines, band, tap_f, tap_b, spread, pre, cd, hidden, bpre, resid, bres,
    g, rc, a1, r1, rz,
    lsem, hs, hr, cs, cr, s1s, s1r, zs, zr, g1s, g1r, gcs, gcr,
):
    lat, lon = lax.axis_index("lat"), lax.axis_index("lon")
    x_hi, yy = lat // 4, lat % 4
    zz, x_lo, core = lon // 4, (lon // 2) % 2, lon % 2
    xx = x_hi * 2 + x_lo

    def at_xy(dx, dy):
        v = (xx + dx) % 4
        return ((v // 2) * 4 + (yy + dy) % 4, zz * 4 + (v % 2) * 2 + core)

    def at_z(d):
        return (lat, ((zz + d) % 8) * 4 + x_lo * 2 + core)

    pair = (lat, zz * 4 + x_lo * 2 + (1 - core))
    right, left = (lon + 1) % 32, (lon + 31) % 32
    has_up, has_down = lat > 0, lat < 7

    loads = [
        pltpu.make_async_copy(fields, x.at[:, 1:5, 0:48], lsem.at[0]),
        pltpu.make_async_copy(edge, vedge, lsem.at[1]),
        pltpu.make_async_copy(filt, vfilt, lsem.at[2]),
        pltpu.make_async_copy(sel_f, vself, lsem.at[3]),
        pltpu.make_async_copy(perm, vperm, lsem.at[4]),
        pltpu.make_async_copy(cot, vcot, lsem.at[5]),
        pltpu.make_async_copy(down, vdown, lsem.at[6]),
        pltpu.make_async_copy(disco, vdisco, lsem.at[7]),
        pltpu.make_async_copy(up, vup, lsem.at[8]),
        pltpu.make_async_copy(sel_b, vselb, lsem.at[9]),
    ]
    for c in loads:
        c.start()

    barrier = pltpu.get_barrier_semaphore()

    def hello(dev):
        pl.semaphore_signal(barrier, inc=1, device_id=dev, device_id_type=MESH)

    hello((lat, right))
    hello((lat, left))

    @pl.when(has_up)
    def _():
        for v in (left, lon, right):
            hello((lat - 1, v))

    @pl.when(has_down)
    def _():
        for v in (left, lon, right):
            hello((lat + 1, v))

    hello(pair)
    for dx, dy in PLANE:
        hello(at_xy(dx, dy))
    for d in RING:
        hello(at_z(d))

    zero48 = jnp.zeros((M, BLOCK, C), BF16)

    @pl.when(lat == 0)
    def _():
        x[:, 0] = zero48
        y[:, 0] = zero48

    @pl.when(lat == 7)
    def _():
        x[:, 5] = zero48
        y[:, 5] = zero48

    def rdma(src, dst, ss, rs, dev):
        return pltpu.make_async_remote_copy(
            src_ref=src, dst_ref=dst, send_sem=ss, recv_sem=rs, device_id=dev, device_id_type=MESH
        )

    def halo(buf, ph):
        st = stage.at[ph]

        def lon_copies():
            return [
                rdma(st.at[0], buf.at[:, 1:5, 48:64], hs.at[ph, 0], hr.at[ph, 0], (lat, right)),
                rdma(st.at[1], buf.at[:, 1:5, 64:80], hs.at[ph, 1], hr.at[ph, 1], (lat, left)),
            ]

        def to_down():
            return [
                rdma(buf.at[:, 4, 0:48], buf.at[:, 0, 0:48], hs.at[ph, 2], hr.at[ph, 2], (lat + 1, lon)),
                rdma(st.at[0, :, 3], buf.at[:, 0, 48:64], hs.at[ph, 3], hr.at[ph, 3], (lat + 1, right)),
                rdma(st.at[1, :, 3], buf.at[:, 0, 64:80], hs.at[ph, 4], hr.at[ph, 4], (lat + 1, left)),
            ]

        def to_up():
            return [
                rdma(buf.at[:, 1, 0:48], buf.at[:, 5, 0:48], hs.at[ph, 5], hr.at[ph, 5], (lat - 1, lon)),
                rdma(st.at[0, :, 0], buf.at[:, 5, 48:64], hs.at[ph, 6], hr.at[ph, 6], (lat - 1, right)),
                rdma(st.at[1, :, 0], buf.at[:, 5, 64:80], hs.at[ph, 7], hr.at[ph, 7], (lat - 1, left)),
            ]

        def start():
            @pl.when(has_down)
            def _():
                for c in to_down():
                    c.start()

            @pl.when(has_up)
            def _():
                for c in to_up():
                    c.start()

            for c in lon_copies():
                c.start()

        def recv():
            for c in lon_copies():
                c.wait_recv()

            @pl.when(has_up)
            def _():
                for c in to_down():
                    c.wait_recv()

            @pl.when(has_down)
            def _():
                for c in to_up():
                    c.wait_recv()

        def sent():
            for c in lon_copies():
                c.wait_send()

            @pl.when(has_down)
            def _():
                for c in to_down():
                    c.wait_send()

            @pl.when(has_up)
            def _():
                for c in to_up():
                    c.wait_send()

        return start, recv, sent

    halo_x = halo(x, 0)
    halo_y = halo(y, 1)

    def own(buf, m):
        return buf[m, 1:5, 0:48].reshape(ROWS * CELLS, C)

    def fill_stage(buf, ph):
        for m in range(M):
            e = dot(vedge[...], own(buf, m)).astype(BF16).reshape(2, PAIRS, 16, C)
            stage[ph, 0, m] = e[0]
            stage[ph, 1, m] = e[1]

    loads[0].wait()
    loads[1].wait()
    fill_stage(x, 0)
    pl.semaphore_wait(
        barrier, 25 + 3 * has_up.astype(jnp.int32) + 3 * has_down.astype(jnp.int32)
    )
    halo_x[0]()

    loads[2].wait()
    filt8[...] = jnp.zeros_like(filt8)
    for n in range(A_TAPS * B_TAPS):
        filt8[n * 8 : n * 8 + K] = vfilt[n].astype(F32)
    first = lat * ROWS - 2
    row_sel = (
        lax.broadcasted_iota(jnp.int32, (16, NLAT), 1)
        == lax.broadcasted_iota(jnp.int32, (16, NLAT), 0) + first
    )
    near = dot(jnp.where(row_sel, 1.0, 0.0).astype(BF16), filt8[...].astype(BF16), ((1,), (1,))).astype(BF16)
    line_row = lax.broadcasted_iota(jnp.int32, (16, K * 256), 0)
    reach = jnp.zeros((16, K * 256), jnp.int32)
    for r in range(12):
        reach = jnp.where(line_row == r, lw[jnp.clip(first + r, 0, NLAT - 1)], reach)
    lane = lax.broadcasted_iota(jnp.int32, (16, K * 256), 1)
    keep = jnp.abs((lane & 31) - 4) <= reach

    def bands(get_line, tap):
        for i in range(ROWS):
            q, i2 = divmod(i, 2)
            parts = []
            for k in range(K):
                line = jnp.broadcast_to(get_line(i, k), (CELLS, 256))
                parts.append(
                    jnp.concatenate(
                        [
                            pltpu.roll(line[:, h * 128 : (h + 1) * 128], 0, 1, stride=1, stride_axis=0)
                            for h in range(2)
                        ],
                        axis=1,
                    )
                )
            band[i2, q * 96 : (q + 1) * 96] = jnp.concatenate(parts, axis=0).astype(BF16)
        res = [dot(band[i2], vperm[i2]) for i2 in range(2)]
        for q in range(PAIRS):
            for k in range(K):
                at = q * 96 + k * CELLS
                both = jnp.concatenate([res[0][at : at + CELLS], res[1][at : at + CELLS]], axis=0)
                tap[q, k * 48 : (k + 1) * 48] = both.astype(BF16)

    loads[3].wait()
    loads[4].wait()
    vline[...] = jnp.where(keep, dot(near, vself[...]), 0.0)
    bands(lambda i, k: vline[i + 2 : i + 3, k * 256 : (k + 1) * 256], tap_f)

    loads[5].wait()
    loads[6].wait()
    cd[...] = dot(vcot[...], vdown[...], ((1,), (1,)))
    loads[9].wait()
    vline[...] = jnp.where(keep, dot(near, vselb[...]), 0.0)
    group = (lax.broadcasted_iota(jnp.int32, (8, K * 256), 1) // 32) % 8
    total = jnp.zeros((8, K * 256), F32)
    for r in range(A_TAPS):
        total = total + jnp.where(group == r, vline[r : r + 8], 0.0)
    lines[...] = total
    bands(lambda i, k: lines[i : i + 1, k * 256 : (k + 1) * 256], tap_b)

    loads[7].wait()
    loads[8].wait()

    def stencil(tap, buf, dst):
        for q in range(PAIRS):
            for m in range(M):
                res = dot(tap[q][:, :NK], buf[m, q : q + 3].reshape(NK, C)).astype(BF16)
                for k in range(K):
                    at = m * 192 + q * 48
                    dst[at : at + 48, k * C : (k + 1) * C] = res[k * 48 : (k + 1) * 48]

    halo_x[1]()
    stencil(tap_f, x, spread)

    for m in range(M):
        mixed = dot(spread[m * 192 : (m + 1) * 192], vdisco[...])
        resid[m * 192 : (m + 1) * 192] = (own(x, m).astype(F32) + mixed).astype(BF16)
    pre[...] = dot(resid[...], vup[...])

    @pl.loop(0, TOK // 16)
    def _(n):
        at = pl.ds(pl.multiple_of(n * 16, 16), 16)
        p = pre[at]
        pp = p * p
        t = jnp.tanh(GELU_SCALE * p * (1.0 + GELU_CUBE * pp))
        h = 0.5 * (1.0 + t)
        hidden[at] = (p * h).astype(BF16)
        slope = h + 0.5 * p * (1.0 - t * t) * GELU_SCALE * (1.0 + 3.0 * GELU_CUBE * pp)
        bpre[at] = (cd[at] * slope).astype(BF16)

    rows0 = ((0,), (0,))

    def put(n, value):
        g[n] = value.astype(BF16).reshape(2, 4, 4, 16, C)

    def core_copy(n):
        return rdma(g.at[n, 1 - core], rc.at[n], cs.at[n], cr.at[n], pair)

    put(0, dot(hidden[...], vcot[...], rows0))
    core_copy(0).start()
    gu = dot(resid[...], bpre[...], rows0)
    put(1, jnp.concatenate([gu[:, :C], gu[:, C:]], axis=0))
    core_copy(1).start()

    def plane_copies(n):
        return [
            rdma(
                a1.at[n, (xx + dx) % 4, (yy + dy) % 4], r1.at[n, i], s1s.at[n, i], s1r.at[n, i],
                at_xy(dx, dy),
            )
            for i, (dx, dy) in enumerate(PLANE)
        ]

    def z_copies(n):
        ref = rz.at[n, zz]
        return [rdma(ref, ref, zs.at[n, i], zr.at[n, i], at_z(d)) for i, d in enumerate(RING)]

    def gather_copies(n):
        ref = o.at[n, core, xx, yy]
        return [
            rdma(ref, ref, g1s.at[n, i], g1r.at[n, i], at_xy(dx, dy))
            for i, (dx, dy) in enumerate(PLANE)
        ]

    def gc_copy(n):
        ref = o.at[n, core]
        return rdma(ref, ref, gcs.at[n], gcr.at[n], pair)

    def start(copies):
        for c in copies:
            c.start()

    def recv(copies):
        for c in copies:
            c.wait_recv()

    def do_core(n):
        core_copy(n).wait_recv()
        a1[n] = (g[n, core].astype(F32) + rc[n].astype(F32)).astype(BF16)
        start(plane_copies(n))

    def do_plane(n):
        recv(plane_copies(n))
        v = a1[n, xx, yy].astype(F32)
        for d in range(15):
            v = v + r1[n, d].astype(F32)
        rz[n, zz] = v.astype(BF16)
        start(z_copies(n))

    def do_z(n):
        recv(z_copies(n))
        v = rz[n, 0].astype(F32)
        for d in range(1, 8):
            v = v + rz[n, d].astype(F32)
        o[n, core, xx, yy] = v.astype(BF16)
        start(gather_copies(n))

    def do_gather(n):
        recv(gather_copies(n))
        gc_copy(n).start()

    br = (vcot[...].astype(F32) + dot(bpre[...], vup[...], ((1,), (1,)))).astype(BF16)
    bres[...] = br
    for m in range(M):
        y[m, 1:5, 0:48] = br[m * 192 : (m + 1) * 192].reshape(PAIRS, 48, C)
    fill_stage(y, 1)
    do_core(0)
    do_core(1)
    for n in range(2):
        put(2 + n, dot(spread[:, n * 512 : (n + 1) * 512], bres[...], rows0))
        core_copy(2 + n).start()

    do_core(2)
    do_core(3)
    halo_y[0]()
    for n in range(4):
        do_plane(n)

    vout[...] = (resid[...].astype(F32) + dot(hidden[...], vdown[...])).astype(BF16)
    for n in range(4):
        do_z(n)
    halo_y[1]()
    stencil(tap_b, y, spread)
    for m in range(M):
        at = slice(m * 192, (m + 1) * 192)
        acc = bres[at].astype(F32)
        for k in range(K):
            acc = acc + dot(
                spread[at, k * C : (k + 1) * C], vdisco[k * C : (k + 1) * C], ((1,), (1,))
            )
        vback[at] = acc.astype(BF16)

    for n in range(4):
        do_gather(n)

    for n in range(4):
        gc_copy(n).wait_recv()

    halo_x[2]()
    halo_y[2]()
    for n in range(4):
        core_copy(n).wait_send()
        for c in plane_copies(n) + z_copies(n) + gather_copies(n):
            c.wait_send()
        gc_copy(n).wait_send()


def finish(o, b, g, out_o, out_b, out_disco, out_up, out_down, wdisco, wup, wdown, sem):
    copies = [
        pltpu.make_async_copy(o, out_o, sem.at[0]),
        pltpu.make_async_copy(b, out_b, sem.at[1]),
        pltpu.make_async_copy(wdisco, out_disco, sem.at[2]),
        pltpu.make_async_copy(wdown, out_down, sem.at[3]),
        pltpu.make_async_copy(wup, out_up, sem.at[4]),
    ]
    copies[0].start()
    copies[1].start()
    wdisco[...] = g[2:].reshape(K * C, C).astype(F32)
    copies[2].start()
    wdown[...] = g[0].reshape(FF, C).astype(F32)
    copies[3].start()
    wup[:, :C] = g[1, 0].reshape(C, C).astype(F32)
    wup[:, C:] = g[1, 1].reshape(C, C).astype(F32)
    copies[4].start()
    for c in copies:
        c.wait()


def per_device(fields, filters, lon_width, disco_weight, up_weight, down_weight, cotangent):
    flat = filters.transpose(1, 2, 3, 0).reshape(A_TAPS * B_TAPS, K, NLAT)
    sel_f, sel_b, perm, edge = [jnp.asarray(v) for v in constants()]
    vspec = pl.BlockSpec(memory_space=pltpu.VMEM)
    anyspec = pl.BlockSpec(memory_space=pl.ANY)
    dma = pltpu.SemaphoreType.DMA
    vm = pltpu.VMEM
    scratch = [
        vm((M, 6, BLOCK, C), BF16),
        vm((M, 6, BLOCK, C), BF16),
        vm((2, 2, M, PAIRS, 16, C), BF16),
        vm((TOK, C), BF16),
        vm((K * C, C), BF16),
        vm((C, FF), BF16),
        vm((FF, C), BF16),
        vm((A_TAPS * B_TAPS, K, NLAT), BF16),
        vm((NF, NLAT), F32),
        vm((NF, K * 256), BF16),
        vm((NF, K * 256), BF16),
        vm((2, 256, 256), BF16),
        vm((2 * PAIRS * 16, ROWS * CELLS), BF16),
        vm((16, K * 256), F32),
        vm((8, K * 256), F32),
        vm((2, PAIRS * 96, 256), BF16),
        vm((PAIRS, 192, 256), BF16),
        vm((PAIRS, 192, 256), BF16),
        vm((TOK, K * C), BF16),
        vm((TOK, FF), F32),
        vm((TOK, FF), F32),
        vm((TOK, FF), BF16),
        vm((TOK, FF), BF16),
        vm((TOK, C), BF16),
        vm((TOK, C), BF16),
        vm((4, 2, 4, 4, 16, C), BF16),
        vm((4, 4, 4, 16, C), BF16),
        vm((4, 4, 4, 16, C), BF16),
        vm((4, 15, 16, C), BF16),
        vm((4, 8, 16, C), BF16),
        dma((10,)),
        dma((2, 8)),
        dma((2, 8)),
        dma((4,)),
        dma((4,)),
        dma((4, 15)),
        dma((4, 15)),
        dma((4, 7)),
        dma((4, 7)),
        dma((4, 15)),
        dma((4, 15)),
        dma((4,)),
        dma((4,)),
    ]
    inner = pl.pallas_call(
        kernel,
        out_shape=(
            vm((TOK, C), BF16),
            vm((TOK, C), BF16),
            vm((4, 2, 4, 4, 16, C), BF16),
        ),
        in_specs=[pl.BlockSpec(memory_space=pltpu.SMEM)] + [pl.BlockSpec(memory_space=pltpu.HBM)] * 10,
        out_specs=[vspec] * 3,
        scratch_shapes=scratch,
        compiler_params=pltpu.CompilerParams(
            collective_id=0, has_side_effects=True, vmem_limit_bytes=62 * 2**20
        ),
    )(
        lon_width,
        fields.reshape(M, PAIRS, 48, C),
        cotangent.reshape(TOK, C),
        disco_weight.reshape(K * C, C),
        up_weight,
        down_weight,
        flat,
        sel_f,
        sel_b,
        perm,
        edge,
    )
    out, back, disco, up, down = pl.pallas_call(
        finish,
        out_shape=(
            jax.ShapeDtypeStruct((TOK, C), BF16),
            jax.ShapeDtypeStruct((TOK, C), BF16),
            jax.ShapeDtypeStruct((K * C, C), F32),
            jax.ShapeDtypeStruct((C, FF), F32),
            jax.ShapeDtypeStruct((FF, C), F32),
        ),
        in_specs=[vspec] * 3,
        out_specs=[pl.BlockSpec(memory_space=pltpu.HBM)] * 5,
        scratch_shapes=[vm((K * C, C), F32), vm((C, FF), F32), vm((FF, C), F32), dma((5,))],
        compiler_params=pltpu.CompilerParams(vmem_limit_bytes=16 * 2**20),
    )(*[pltpu.with_memory_space_constraint(v, pltpu.VMEM) for v in inner])
    shape = fields.shape
    return out.reshape(shape), back.reshape(shape), disco.reshape(K, C, C), up, down


def solution(mesh):
    placed = (P(None, "lat", "lon", None), P(), P(), P(), P(), P(), P(None, "lat", "lon", None))
    return jax.shard_map(
        per_device,
        mesh=mesh,
        in_specs=placed,
        out_specs=(P(None, "lat", "lon", None), P(None, "lat", "lon", None), P(), P(), P()),
        check_vma=False,
    )
```

```python
import functools

import jax
import jax.numpy as jnp
import numpy as np
from jax import lax
from jax.experimental import pallas as pl
from jax.experimental.pallas import tpu as pltpu
from jax.sharding import PartitionSpec as P

GELU_SCALE = 0.7978845608028654
GELU_CUBE = 0.044715
MESH = pl.DeviceIdType.MESH
F32 = jnp.float32
BF16 = jnp.bfloat16

M, ROWS, CELLS, C, FF, K = 2, 8, 24, 256, 512, 4
NLAT = 64
A_TAPS, B_TAPS = 5, 9
PAIRS = ROWS // 2
TOK = M * ROWS * CELLS
BLOCK = 80
NK = 3 * BLOCK
NF = A_TAPS * B_TAPS * 8
PLANE = sorted(
    [(dx, dy) for dx in range(4) for dy in range(4) if dx or dy],
    key=lambda t: (-min(t[0], 4 - t[0]) - min(t[1], 4 - t[1]), t),
)
RING = (4, 3, 5, 2, 6, 1, 7)


def constants():
    sel_f = np.zeros((NF, K * 256), np.float32)
    sel_b = np.zeros((NF, K * 256), np.float32)
    for a in range(A_TAPS):
        for b in range(B_TAPS):
            for k in range(K):
                s = (a * B_TAPS + b) * 8 + k
                sel_f[s, k * 256 + a * 32 + b] = 1
                sel_b[s, k * 256 + (4 - a) * 32 + 8 - b] = 1
    perm = np.zeros((2, 256, 256), np.float32)
    for i2 in range(2):
        for a in range(A_TAPS):
            p, r2 = divmod(i2 + a, 2)
            for jj in range(32):
                if jj < 4:
                    col = p * BLOCK + 48 + r2 * 4 + jj
                elif jj < 28:
                    col = p * BLOCK + r2 * CELLS + jj - 4
                else:
                    col = p * BLOCK + 64 + r2 * 4 + jj - 28
                perm[i2, a * 32 + jj, col] = 1
    edge = np.zeros((2 * PAIRS * 16, ROWS * CELLS), np.float32)
    for side in range(2):
        for q in range(PAIRS):
            for r2 in range(2):
                for j in range(4):
                    cell = (CELLS - 4 + j) if side == 0 else j
                    edge[(side * PAIRS + q) * 16 + r2 * 4 + j, (q * 2 + r2) * CELLS + cell] = 1
    return [x.astype(jnp.bfloat16) for x in (sel_f, sel_b, perm, edge)]


def dot(a, b, dims=((1,), (0,))):
    return lax.dot_general(a, b, (dims, ((), ())), preferred_element_type=F32)


def kernel(
    lw, fields, cot, disco, up, down, filt, sel_f, sel_b, perm, edge,
    vout, vback, disco_out, up_out, down_out,
    x, y, stage, vcot, vdisco, vup, vdown, vfilt, filt8, vself, vselb, vperm, vedge,
    vline, lines, band, tap_f, tap_b, spread, pre, cd, hidden, bpre, resid, bres,
    g, rc, a1, r1, rz, o,
    lsem, hs, hr, cs, cr, s1s, s1r, zs, zr, g1s, g1r, gcs, gcr,
):
    lat, lon = lax.axis_index("lat"), lax.axis_index("lon")
    x_hi, yy = lat // 4, lat % 4
    zz, x_lo, core = lon // 4, (lon // 2) % 2, lon % 2
    xx = x_hi * 2 + x_lo

    def at_xy(dx, dy):
        v = (xx + dx) % 4
        return ((v // 2) * 4 + (yy + dy) % 4, zz * 4 + (v % 2) * 2 + core)

    def at_z(d):
        return (lat, ((zz + d) % 8) * 4 + x_lo * 2 + core)

    pair = (lat, zz * 4 + x_lo * 2 + (1 - core))
    right, left = (lon + 1) % 32, (lon + 31) % 32
    has_up, has_down = lat > 0, lat < 7

    loads = [
        pltpu.make_async_copy(fields, x.at[:, 1:5, 0:48], lsem.at[0]),
        pltpu.make_async_copy(edge, vedge, lsem.at[1]),
        pltpu.make_async_copy(filt, vfilt, lsem.at[2]),
        pltpu.make_async_copy(sel_f, vself, lsem.at[3]),
        pltpu.make_async_copy(perm, vperm, lsem.at[4]),
        pltpu.make_async_copy(cot, vcot, lsem.at[5]),
        pltpu.make_async_copy(down, vdown, lsem.at[6]),
        pltpu.make_async_copy(disco, vdisco, lsem.at[7]),
        pltpu.make_async_copy(up, vup, lsem.at[8]),
        pltpu.make_async_copy(sel_b, vselb, lsem.at[9]),
    ]
    for c in loads:
        c.start()

    barrier = pltpu.get_barrier_semaphore()

    def hello(dev):
        pl.semaphore_signal(barrier, inc=1, device_id=dev, device_id_type=MESH)

    hello((lat, right))
    hello((lat, left))

    @pl.when(has_up)
    def _():
        for v in (left, lon, right):
            hello((lat - 1, v))

    @pl.when(has_down)
    def _():
        for v in (left, lon, right):
            hello((lat + 1, v))

    hello(pair)
    for dx, dy in PLANE:
        hello(at_xy(dx, dy))
    for d in RING:
        hello(at_z(d))

    zero48 = jnp.zeros((M, BLOCK, C), BF16)

    @pl.when(lat == 0)
    def _():
        x[:, 0] = zero48
        y[:, 0] = zero48

    @pl.when(lat == 7)
    def _():
        x[:, 5] = zero48
        y[:, 5] = zero48

    def rdma(src, dst, ss, rs, dev):
        return pltpu.make_async_remote_copy(
            src_ref=src, dst_ref=dst, send_sem=ss, recv_sem=rs, device_id=dev, device_id_type=MESH
        )

    def halo(buf, ph):
        st = stage.at[ph]

        def lon_copies():
            return [
                rdma(st.at[0], buf.at[:, 1:5, 48:64], hs.at[ph, 0], hr.at[ph, 0], (lat, right)),
                rdma(st.at[1], buf.at[:, 1:5, 64:80], hs.at[ph, 1], hr.at[ph, 1], (lat, left)),
            ]

        def to_down():
            return [
                rdma(buf.at[:, 4, 0:48], buf.at[:, 0, 0:48], hs.at[ph, 2], hr.at[ph, 2], (lat + 1, lon)),
                rdma(st.at[0, :, 3], buf.at[:, 0, 48:64], hs.at[ph, 3], hr.at[ph, 3], (lat + 1, right)),
                rdma(st.at[1, :, 3], buf.at[:, 0, 64:80], hs.at[ph, 4], hr.at[ph, 4], (lat + 1, left)),
            ]

        def to_up():
            return [
                rdma(buf.at[:, 1, 0:48], buf.at[:, 5, 0:48], hs.at[ph, 5], hr.at[ph, 5], (lat - 1, lon)),
                rdma(st.at[0, :, 0], buf.at[:, 5, 48:64], hs.at[ph, 6], hr.at[ph, 6], (lat - 1, right)),
                rdma(st.at[1, :, 0], buf.at[:, 5, 64:80], hs.at[ph, 7], hr.at[ph, 7], (lat - 1, left)),
            ]

        def start():
            @pl.when(has_down)
            def _():
                for c in to_down():
                    c.start()

            @pl.when(has_up)
            def _():
                for c in to_up():
                    c.start()

            for c in lon_copies():
                c.start()

        def recv():
            for c in lon_copies():
                c.wait_recv()

            @pl.when(has_up)
            def _():
                for c in to_down():
                    c.wait_recv()

            @pl.when(has_down)
            def _():
                for c in to_up():
                    c.wait_recv()

        def sent():
            for c in lon_copies():
                c.wait_send()

            @pl.when(has_down)
            def _():
                for c in to_down():
                    c.wait_send()

            @pl.when(has_up)
            def _():
                for c in to_up():
                    c.wait_send()

        return start, recv, sent

    halo_x = halo(x, 0)
    halo_y = halo(y, 1)

    def own(buf, m):
        return buf[m, 1:5, 0:48].reshape(ROWS * CELLS, C)

    def fill_stage(buf, ph):
        for m in range(M):
            e = dot(vedge[...], own(buf, m)).astype(BF16).reshape(2, PAIRS, 16, C)
            stage[ph, 0, m] = e[0]
            stage[ph, 1, m] = e[1]

    loads[0].wait()
    loads[1].wait()
    fill_stage(x, 0)
    pl.semaphore_wait(
        barrier, 25 + 3 * has_up.astype(jnp.int32) + 3 * has_down.astype(jnp.int32)
    )
    halo_x[0]()

    loads[2].wait()
    filt8[...] = jnp.zeros_like(filt8)
    for n in range(A_TAPS * B_TAPS):
        filt8[n * 8 : n * 8 + K] = vfilt[n].astype(F32)
    first = lat * ROWS - 2
    row_sel = (
        lax.broadcasted_iota(jnp.int32, (16, NLAT), 1)
        == lax.broadcasted_iota(jnp.int32, (16, NLAT), 0) + first
    )
    near = dot(jnp.where(row_sel, 1.0, 0.0).astype(BF16), filt8[...].astype(BF16), ((1,), (1,))).astype(BF16)
    line_row = lax.broadcasted_iota(jnp.int32, (16, K * 256), 0)
    reach = jnp.zeros((16, K * 256), jnp.int32)
    for r in range(12):
        reach = jnp.where(line_row == r, lw[jnp.clip(first + r, 0, NLAT - 1)], reach)
    lane = lax.broadcasted_iota(jnp.int32, (16, K * 256), 1)
    keep = jnp.abs((lane & 31) - 4) <= reach

    def bands(get_line, tap):
        for i in range(ROWS):
            q, i2 = divmod(i, 2)
            parts = []
            for k in range(K):
                line = jnp.broadcast_to(get_line(i, k), (CELLS, 256))
                parts.append(
                    jnp.concatenate(
                        [
                            pltpu.roll(line[:, h * 128 : (h + 1) * 128], 0, 1, stride=1, stride_axis=0)
                            for h in range(2)
                        ],
                        axis=1,
                    )
                )
            band[i2, q * 96 : (q + 1) * 96] = jnp.concatenate(parts, axis=0).astype(BF16)
        res = [dot(band[i2], vperm[i2]) for i2 in range(2)]
        for q in range(PAIRS):
            for k in range(K):
                at = q * 96 + k * CELLS
                both = jnp.concatenate([res[0][at : at + CELLS], res[1][at : at + CELLS]], axis=0)
                tap[q, k * 48 : (k + 1) * 48] = both.astype(BF16)

    loads[3].wait()
    loads[4].wait()
    vline[...] = jnp.where(keep, dot(near, vself[...]), 0.0)
    bands(lambda i, k: vline[i + 2 : i + 3, k * 256 : (k + 1) * 256], tap_f)

    loads[5].wait()
    loads[6].wait()
    cd[...] = dot(vcot[...], vdown[...], ((1,), (1,)))
    loads[9].wait()
    loads[7].wait()
    loads[8].wait()

    def stencil(tap, buf, dst):
        for q in range(PAIRS):
            for m in range(M):
                res = dot(tap[q][:, :NK], buf[m, q : q + 3].reshape(NK, C)).astype(BF16)
                for k in range(K):
                    at = m * 192 + q * 48
                    dst[at : at + 48, k * C : (k + 1) * C] = res[k * 48 : (k + 1) * 48]

    halo_x[1]()
    stencil(tap_f, x, spread)

    for m in range(M):
        mixed = dot(spread[m * 192 : (m + 1) * 192], vdisco[...])
        resid[m * 192 : (m + 1) * 192] = (own(x, m).astype(F32) + mixed).astype(BF16)
    pre[...] = dot(resid[...], vup[...])

    @pl.loop(0, TOK // 16)
    def _(n):
        at = pl.ds(pl.multiple_of(n * 16, 16), 16)
        p = pre[at]
        pp = p * p
        t = jnp.tanh(GELU_SCALE * p * (1.0 + GELU_CUBE * pp))
        h = 0.5 * (1.0 + t)
        hidden[at] = (p * h).astype(BF16)
        slope = h + 0.5 * p * (1.0 - t * t) * GELU_SCALE * (1.0 + 3.0 * GELU_CUBE * pp)
        bpre[at] = (cd[at] * slope).astype(BF16)

    rows0 = ((0,), (0,))

    def put(n, value):
        g[n] = value.astype(BF16).reshape(2, 4, 4, 16, C)

    def core_copy(n):
        return rdma(g.at[n, 1 - core], rc.at[n], cs.at[n], cr.at[n], pair)

    put(0, dot(hidden[...], vcot[...], rows0))
    core_copy(0).start()
    gu = dot(resid[...], bpre[...], rows0)
    put(1, jnp.concatenate([gu[:, :C], gu[:, C:]], axis=0))
    core_copy(1).start()

    def plane_copies(n):
        return [
            rdma(
                a1.at[n, (xx + dx) % 4, (yy + dy) % 4], r1.at[n, i], s1s.at[n], s1r.at[n],
                at_xy(dx, dy),
            )
            for i, (dx, dy) in enumerate(PLANE)
        ]

    def z_copies(n):
        ref = rz.at[n, zz]
        return [rdma(ref, ref, zs.at[n], zr.at[n], at_z(d)) for d in RING]

    def gather_copies(n):
        ref = o.at[n, core, xx, yy]
        return [
            rdma(ref, ref, g1s.at[n], g1r.at[n], at_xy(dx, dy))
            for dx, dy in PLANE
        ]

    def gc_copy(n):
        ref = o.at[n, core]
        return rdma(ref, ref, gcs.at[n], gcr.at[n], pair)

    def start(copies):
        for c in copies:
            c.start()

    def wait_all(blocks, sem):
        ref = r1.at[0, 0:blocks]
        pltpu.make_async_copy(ref, ref, sem).wait()

    def do_core(n):
        core_copy(n).wait_recv()
        a1[n] = (g[n, core].astype(F32) + rc[n].astype(F32)).astype(BF16)
        start(plane_copies(n))

    def do_plane(n):
        wait_all(15, s1r.at[n])
        v = a1[n, xx, yy].astype(F32)
        for d in range(15):
            v = v + r1[n, d].astype(F32)
        rz[n, zz] = v.astype(BF16)
        start(z_copies(n))

    def do_z(n):
        wait_all(7, zr.at[n])
        v = rz[n, 0].astype(F32)
        for d in range(1, 8):
            v = v + rz[n, d].astype(F32)
        o[n, core, xx, yy] = v.astype(BF16)
        start(gather_copies(n))

    def do_gather(n):
        wait_all(15, g1r.at[n])
        gc_copy(n).start()

    br = (vcot[...].astype(F32) + dot(bpre[...], vup[...], ((1,), (1,)))).astype(BF16)
    bres[...] = br
    for m in range(M):
        y[m, 1:5, 0:48] = br[m * 192 : (m + 1) * 192].reshape(PAIRS, 48, C)
    fill_stage(y, 1)
    do_core(0)
    do_core(1)
    for n in range(2):
        put(2 + n, dot(spread[:, n * 512 : (n + 1) * 512], bres[...], rows0))
        core_copy(2 + n).start()

    do_core(2)
    do_core(3)
    halo_y[0]()
    vline[...] = jnp.where(keep, dot(near, vselb[...]), 0.0)
    group = (lax.broadcasted_iota(jnp.int32, (8, K * 256), 1) // 32) % 8
    total = jnp.zeros((8, K * 256), F32)
    for r in range(A_TAPS):
        total = total + jnp.where(group == r, vline[r : r + 8], 0.0)
    lines[...] = total
    bands(lambda i, k: lines[i : i + 1, k * 256 : (k + 1) * 256], tap_b)

    for n in range(4):
        do_plane(n)

    vout[...] = (resid[...].astype(F32) + dot(hidden[...], vdown[...])).astype(BF16)
    halo_x[2]()
    halo_y[2]()
    for n in range(4):
        core_copy(n).wait_send()
        wait_all(15, s1s.at[n])
    for n in range(4):
        do_z(n)
    for n in range(4):
        wait_all(7, zs.at[n])
    halo_y[1]()
    stencil(tap_b, y, spread)
    for m in range(M):
        at = slice(m * 192, (m + 1) * 192)
        acc = bres[at].astype(F32)
        for k in range(K):
            acc = acc + dot(
                spread[at, k * C : (k + 1) * C], vdisco[k * C : (k + 1) * C], ((1,), (1,))
            )
        vback[at] = acc.astype(BF16)

    for n in range(4):
        do_gather(n)

    for n in range(4):
        wait_all(15, g1s.at[n])
    for n in range(4):
        gc_copy(n).wait_recv()
        whole = o[n].astype(F32)
        if n == 0:
            down_out[...] = whole.reshape(FF, C)
        elif n == 1:
            up_out[:, :C] = whole[0].reshape(C, C)
            up_out[:, C:] = whole[1].reshape(C, C)
        else:
            disco_out[(n - 2) * 512 : (n - 1) * 512] = whole.reshape(512, C)
    for n in range(4):
        gc_copy(n).wait_send()


def finish(*refs):
    sem = refs[10]
    copies = [pltpu.make_async_copy(refs[n], refs[5 + n], sem.at[n]) for n in (2, 3, 4, 0, 1)]
    for c in copies:
        c.start()
    for c in copies:
        c.wait()


def per_device(fields, filters, lon_width, disco_weight, up_weight, down_weight, cotangent):
    flat = filters.transpose(1, 2, 3, 0).reshape(A_TAPS * B_TAPS, K, NLAT)
    sel_f, sel_b, perm, edge = [jnp.asarray(v) for v in constants()]
    vspec = pl.BlockSpec(memory_space=pltpu.VMEM)
    anyspec = pl.BlockSpec(memory_space=pl.ANY)
    dma = pltpu.SemaphoreType.DMA
    vm = pltpu.VMEM
    scratch = [
        vm((M, 6, BLOCK, C), BF16),
        vm((M, 6, BLOCK, C), BF16),
        vm((2, 2, M, PAIRS, 16, C), BF16),
        vm((TOK, C), BF16),
        vm((K * C, C), BF16),
        vm((C, FF), BF16),
        vm((FF, C), BF16),
        vm((A_TAPS * B_TAPS, K, NLAT), BF16),
        vm((NF, NLAT), F32),
        vm((NF, K * 256), BF16),
        vm((NF, K * 256), BF16),
        vm((2, 256, 256), BF16),
        vm((2 * PAIRS * 16, ROWS * CELLS), BF16),
        vm((16, K * 256), F32),
        vm((8, K * 256), F32),
        vm((2, PAIRS * 96, 256), BF16),
        vm((PAIRS, 192, 256), BF16),
        vm((PAIRS, 192, 256), BF16),
        vm((TOK, K * C), BF16),
        vm((TOK, FF), F32),
        vm((TOK, FF), F32),
        vm((TOK, FF), BF16),
        vm((TOK, FF), BF16),
        vm((TOK, C), BF16),
        vm((TOK, C), BF16),
        vm((4, 2, 4, 4, 16, C), BF16),
        vm((4, 4, 4, 16, C), BF16),
        vm((4, 4, 4, 16, C), BF16),
        vm((4, 15, 16, C), BF16),
        vm((4, 8, 16, C), BF16),
        vm((4, 2, 4, 4, 16, C), BF16),
        dma((10,)),
        dma((2, 8)),
        dma((2, 8)),
        dma((4,)),
        dma((4,)),
        dma((4,)),
        dma((4,)),
        dma((4,)),
        dma((4,)),
        dma((4,)),
        dma((4,)),
        dma((4,)),
        dma((4,)),
    ]
    results = (((TOK, C), BF16), ((TOK, C), BF16), ((K * C, C), F32), ((C, FF), F32), ((FF, C), F32))
    inner = pl.pallas_call(
        kernel,
        out_shape=[vm(*r) for r in results],
        in_specs=[pl.BlockSpec(memory_space=pltpu.SMEM)] + [pl.BlockSpec(memory_space=pltpu.HBM)] * 10,
        out_specs=[vspec] * 5,
        scratch_shapes=scratch,
        compiler_params=pltpu.CompilerParams(
            collective_id=0, has_side_effects=True, vmem_limit_bytes=60 * 2**20
        ),
    )(
        lon_width,
        fields.reshape(M, PAIRS, 48, C),
        cotangent.reshape(TOK, C),
        disco_weight.reshape(K * C, C),
        up_weight,
        down_weight,
        flat,
        sel_f,
        sel_b,
        perm,
        edge,
    )
    out, back, disco, up, down = pl.pallas_call(
        finish,
        out_shape=[jax.ShapeDtypeStruct(*r) for r in results],
        in_specs=[vspec] * 5,
        out_specs=[pl.BlockSpec(memory_space=pltpu.HBM)] * 5,
        scratch_shapes=[dma((5,))],
        compiler_params=pltpu.CompilerParams(vmem_limit_bytes=16 * 2**20),
    )(*[pltpu.with_memory_space_constraint(v, pltpu.VMEM) for v in inner])
    shape = fields.shape
    return out.reshape(shape), back.reshape(shape), disco.reshape(K, C, C), up, down


def solution(mesh):
    placed = (P(None, "lat", "lon", None), P(), P(), P(), P(), P(), P(None, "lat", "lon", None))
    return jax.shard_map(
        per_device,
        mesh=mesh,
        in_specs=placed,
        out_specs=(P(None, "lat", "lon", None), P(None, "lat", "lon", None), P(), P(), P()),
        check_vma=False,
    )
```

```python
import functools

import jax
import jax.numpy as jnp
import numpy as np
from jax import lax
from jax.experimental import pallas as pl
from jax.experimental.pallas import tpu as pltpu
from jax.sharding import PartitionSpec as P

GELU_SCALE = 0.7978845608028654
GELU_CUBE = 0.044715
MESH = pl.DeviceIdType.MESH
F32 = jnp.float32
BF16 = jnp.bfloat16

M, ROWS, CELLS, C, FF, K = 2, 8, 24, 256, 512, 4
NLAT = 64
A_TAPS, B_TAPS = 5, 9
PAIRS = ROWS // 2
TOK = M * ROWS * CELLS
OWN, SIDES = 48, 32
NK = 3 * (OWN + SIDES)
NF = A_TAPS * B_TAPS * 8
PLANE = sorted(
    [(dx, dy) for dx in range(4) for dy in range(4) if dx or dy],
    key=lambda t: (-min(t[0], 4 - t[0]) - min(t[1], 4 - t[1]), t),
)
RING = (4, 3, 5, 2, 6, 1, 7)


def constants():
    sel_f = np.zeros((NF, K * 256), np.float32)
    sel_b = np.zeros((NF, K * 256), np.float32)
    for a in range(A_TAPS):
        for b in range(B_TAPS):
            for k in range(K):
                s = (a * B_TAPS + b) * 8 + k
                sel_f[s, k * 256 + a * 32 + b] = 1
                sel_b[s, k * 256 + (4 - a) * 32 + 8 - b] = 1
    perm = np.zeros((2, 256, M * 256), np.float32)
    for i2 in range(2):
        for a in range(A_TAPS):
            p, r2 = divmod(i2 + a, 2)
            for jj in range(32):
                for m in range(M):
                    side = 3 * OWN + p * SIDES + m * 8 + r2 * 4
                    if jj < 4:
                        col = side + jj
                    elif jj < 28:
                        col = p * OWN + r2 * CELLS + jj - 4
                    else:
                        col = side + 16 + jj - 28
                    perm[i2, a * 32 + jj, m * 256 + col] = 1
    edge = np.zeros((2 * PAIRS * 16, TOK), np.float32)
    for side in range(2):
        for q in range(PAIRS):
            for m in range(M):
                for r2 in range(2):
                    for j in range(4):
                        cell = (CELLS - 4 + j) if side == 0 else j
                        token = ((m * PAIRS + q) * 2 + r2) * CELLS + cell
                        edge[(side * PAIRS + q) * 16 + m * 8 + r2 * 4 + j, token] = 1
    return [x.astype(jnp.bfloat16) for x in (sel_f, sel_b, perm, edge)]


def dot(a, b, dims=((1,), (0,))):
    return lax.dot_general(a, b, (dims, ((), ())), preferred_element_type=F32)


def kernel(
    lw, fields, cot, disco, up, down, filt, sel_f, sel_b, perm, edge,
    vout, vback, disco_out, up_out, down_out,
    x, y, xs, ys, stage, vcot, vdisco, vup, vdown, vfilt, filt8, vself, vselb, vperm, vedge,
    vline, lines, band, tap_f, tap_b, spread, pre, cd, hidden, bpre, resid, bres,
    g, rc, a1, r1, rz, o,
    lsem, hs, hr, cs, cr, s1s, s1r, zs, zr, g1s, g1r, gcs, gcr,
):
    lat, lon = lax.axis_index("lat"), lax.axis_index("lon")
    x_hi, yy = lat // 4, lat % 4
    zz, x_lo, core = lon // 4, (lon // 2) % 2, lon % 2
    xx = x_hi * 2 + x_lo

    def at_xy(dx, dy):
        v = (xx + dx) % 4
        return ((v // 2) * 4 + (yy + dy) % 4, zz * 4 + (v % 2) * 2 + core)

    def at_z(d):
        return (lat, ((zz + d) % 8) * 4 + x_lo * 2 + core)

    pair = (lat, zz * 4 + x_lo * 2 + (1 - core))
    right, left = (lon + 1) % 32, (lon + 31) % 32
    has_up, has_down = lat > 0, lat < 7

    loads = [
        pltpu.make_async_copy(fields, x.at[:, 1:5], lsem.at[0]),
        pltpu.make_async_copy(edge, vedge, lsem.at[1]),
        pltpu.make_async_copy(filt, vfilt, lsem.at[2]),
        pltpu.make_async_copy(sel_f, vself, lsem.at[3]),
        pltpu.make_async_copy(perm, vperm, lsem.at[4]),
        pltpu.make_async_copy(cot, vcot, lsem.at[5]),
        pltpu.make_async_copy(down, vdown, lsem.at[6]),
        pltpu.make_async_copy(disco, vdisco, lsem.at[7]),
        pltpu.make_async_copy(up, vup, lsem.at[8]),
        pltpu.make_async_copy(sel_b, vselb, lsem.at[9]),
    ]
    for c in loads:
        c.start()

    barrier = pltpu.get_barrier_semaphore()

    def hello(dev):
        pl.semaphore_signal(barrier, inc=1, device_id=dev, device_id_type=MESH)

    hello((lat, right))
    hello((lat, left))

    @pl.when(has_up)
    def _():
        for v in (left, lon, right):
            hello((lat - 1, v))

    @pl.when(has_down)
    def _():
        for v in (left, lon, right):
            hello((lat + 1, v))

    hello(pair)
    for dx, dy in PLANE:
        hello(at_xy(dx, dy))
    for d in RING:
        hello(at_z(d))

    def clear(n):
        for buf, sides in ((x, xs), (y, ys)):
            buf[:, n] = jnp.zeros((M, OWN, C), BF16)
            sides[n] = jnp.zeros((SIDES, C), BF16)

    @pl.when(lat == 0)
    def _():
        clear(0)

    @pl.when(lat == 7)
    def _():
        clear(5)

    def rdma(src, dst, ss, rs, dev):
        return pltpu.make_async_remote_copy(
            src_ref=src, dst_ref=dst, send_sem=ss, recv_sem=rs, device_id=dev, device_id_type=MESH
        )

    def halo(buf, sides, ph):
        st = stage.at[ph]

        def lon_copies():
            return [
                rdma(st.at[0], sides.at[1:5, 0:16], hs.at[ph, 0], hr.at[ph, 0], (lat, right)),
                rdma(st.at[1], sides.at[1:5, 16:32], hs.at[ph, 1], hr.at[ph, 1], (lat, left)),
            ]

        def to_down():
            return [
                rdma(buf.at[:, 4], buf.at[:, 0], hs.at[ph, 2], hr.at[ph, 2], (lat + 1, lon)),
                rdma(st.at[0, 3], sides.at[0, 0:16], hs.at[ph, 3], hr.at[ph, 3], (lat + 1, right)),
                rdma(st.at[1, 3], sides.at[0, 16:32], hs.at[ph, 4], hr.at[ph, 4], (lat + 1, left)),
            ]

        def to_up():
            return [
                rdma(buf.at[:, 1], buf.at[:, 5], hs.at[ph, 5], hr.at[ph, 5], (lat - 1, lon)),
                rdma(st.at[0, 0], sides.at[5, 0:16], hs.at[ph, 6], hr.at[ph, 6], (lat - 1, right)),
                rdma(st.at[1, 0], sides.at[5, 16:32], hs.at[ph, 7], hr.at[ph, 7], (lat - 1, left)),
            ]

        def start():
            @pl.when(has_down)
            def _():
                for c in to_down():
                    c.start()

            @pl.when(has_up)
            def _():
                for c in to_up():
                    c.start()

            for c in lon_copies():
                c.start()

        def recv():
            for c in lon_copies():
                c.wait_recv()

            @pl.when(has_up)
            def _():
                for c in to_down():
                    c.wait_recv()

            @pl.when(has_down)
            def _():
                for c in to_up():
                    c.wait_recv()

        def sent():
            for c in lon_copies():
                c.wait_send()

            @pl.when(has_down)
            def _():
                for c in to_down():
                    c.wait_send()

            @pl.when(has_up)
            def _():
                for c in to_up():
                    c.wait_send()

        return start, recv, sent

    halo_x = halo(x, xs, 0)
    halo_y = halo(y, ys, 1)

    def own(buf, m):
        return buf[m, 1:5].reshape(ROWS * CELLS, C)

    def fill_stage(buf, ph):
        e = dot(vedge[...], buf[:, 1:5].reshape(TOK, C)).astype(BF16)
        stage[ph] = e.reshape(2, PAIRS, 16, C)

    loads[0].wait()
    loads[1].wait()
    fill_stage(x, 0)
    pl.semaphore_wait(
        barrier, 25 + 3 * has_up.astype(jnp.int32) + 3 * has_down.astype(jnp.int32)
    )
    halo_x[0]()

    loads[2].wait()
    filt8[...] = jnp.zeros_like(filt8)
    for n in range(A_TAPS * B_TAPS):
        filt8[n * 8 : n * 8 + K] = vfilt[n].astype(F32)
    first = lat * ROWS - 2
    row_sel = (
        lax.broadcasted_iota(jnp.int32, (16, NLAT), 1)
        == lax.broadcasted_iota(jnp.int32, (16, NLAT), 0) + first
    )
    near = dot(jnp.where(row_sel, 1.0, 0.0).astype(BF16), filt8[...].astype(BF16), ((1,), (1,))).astype(BF16)
    line_row = lax.broadcasted_iota(jnp.int32, (16, K * 256), 0)
    reach = jnp.zeros((16, K * 256), jnp.int32)
    for r in range(12):
        reach = jnp.where(line_row == r, lw[jnp.clip(first + r, 0, NLAT - 1)], reach)
    lane = lax.broadcasted_iota(jnp.int32, (16, K * 256), 1)
    keep = jnp.abs((lane & 31) - 4) <= reach

    def bands(get_line, tap):
        for i in range(ROWS):
            q, i2 = divmod(i, 2)
            parts = []
            for k in range(K):
                line = jnp.broadcast_to(get_line(i, k), (CELLS, 256))
                parts.append(
                    jnp.concatenate(
                        [
                            pltpu.roll(line[:, h * 128 : (h + 1) * 128], 0, 1, stride=1, stride_axis=0)
                            for h in range(2)
                        ],
                        axis=1,
                    )
                )
            band[i2, q * 96 : (q + 1) * 96] = jnp.concatenate(parts, axis=0).astype(BF16)
        res = [dot(band[i2], vperm[i2]) for i2 in range(2)]
        for q in range(PAIRS):
            for k in range(K):
                at = q * 96 + k * CELLS
                both = jnp.concatenate([res[0][at : at + CELLS], res[1][at : at + CELLS]], axis=0)
                for m in range(M):
                    tap[m, q, k * 48 : (k + 1) * 48] = both[:, m * 256 : (m + 1) * 256].astype(BF16)

    loads[3].wait()
    loads[4].wait()
    vline[...] = jnp.where(keep, dot(near, vself[...]), 0.0)
    bands(lambda i, k: vline[i + 2 : i + 3, k * 256 : (k + 1) * 256], tap_f)

    loads[5].wait()
    loads[6].wait()
    cd[...] = dot(vcot[...], vdown[...], ((1,), (1,)))
    loads[9].wait()
    loads[7].wait()
    loads[8].wait()

    def stencil(tap, buf, sides, dst):
        for q in range(PAIRS):
            for m in range(M):
                window = jnp.concatenate(
                    [buf[m, q : q + 3].reshape(3 * OWN, C), sides[q : q + 3].reshape(3 * SIDES, C)], axis=0
                )
                res = dot(tap[m, q][:, :NK], window).astype(BF16)
                for k in range(K):
                    at = m * 192 + q * 48
                    dst[at : at + 48, k * C : (k + 1) * C] = res[k * 48 : (k + 1) * 48]

    halo_x[1]()
    stencil(tap_f, x, xs, spread)

    for m in range(M):
        mixed = dot(spread[m * 192 : (m + 1) * 192], vdisco[...])
        resid[m * 192 : (m + 1) * 192] = (own(x, m).astype(F32) + mixed).astype(BF16)
    pre[...] = dot(resid[...], vup[...])

    @pl.loop(0, TOK // 16)
    def _(n):
        at = pl.ds(pl.multiple_of(n * 16, 16), 16)
        p = pre[at]
        pp = p * p
        t = jnp.tanh(GELU_SCALE * p * (1.0 + GELU_CUBE * pp))
        h = 0.5 * (1.0 + t)
        hidden[at] = (p * h).astype(BF16)
        slope = h + 0.5 * p * (1.0 - t * t) * GELU_SCALE * (1.0 + 3.0 * GELU_CUBE * pp)
        bpre[at] = (cd[at] * slope).astype(BF16)

    rows0 = ((0,), (0,))

    def put(n, value):
        g[n] = value.astype(BF16).reshape(2, 4, 4, 16, C)

    def core_copy(n):
        return rdma(g.at[n, 1 - core], rc.at[n], cs.at[n], cr.at[n], pair)

    put(0, dot(hidden[...], vcot[...], rows0))
    core_copy(0).start()
    gu = dot(resid[...], bpre[...], rows0)
    put(1, jnp.concatenate([gu[:, :C], gu[:, C:]], axis=0))
    core_copy(1).start()

    def plane_copies(n):
        return [
            rdma(
                a1.at[n, (xx + dx) % 4, (yy + dy) % 4], r1.at[n, i], s1s.at[n], s1r.at[n],
                at_xy(dx, dy),
            )
            for i, (dx, dy) in enumerate(PLANE)
        ]

    def z_copies(n):
        ref = rz.at[n, zz]
        return [rdma(ref, ref, zs.at[n], zr.at[n], at_z(d)) for d in RING]

    def gather_copies(n):
        ref = o.at[n, core, xx, yy]
        return [
            rdma(ref, ref, g1s.at[n], g1r.at[n], at_xy(dx, dy))
            for dx, dy in PLANE
        ]

    def gc_copy(n):
        ref = o.at[n, core]
        return rdma(ref, ref, gcs.at[n], gcr.at[n], pair)

    def start(copies):
        for c in copies:
            c.start()

    def wait_all(blocks, sem):
        ref = r1.at[0, 0:blocks]
        pltpu.make_async_copy(ref, ref, sem).wait()

    def do_core(n):
        core_copy(n).wait_recv()
        a1[n] = (g[n, core].astype(F32) + rc[n].astype(F32)).astype(BF16)
        start(plane_copies(n))

    def do_plane(n):
        wait_all(15, s1r.at[n])
        v = a1[n, xx, yy].astype(F32)
        for d in range(15):
            v = v + r1[n, d].astype(F32)
        rz[n, zz] = v.astype(BF16)
        start(z_copies(n))

    def do_z(n):
        wait_all(7, zr.at[n])
        v = rz[n, 0].astype(F32)
        for d in range(1, 8):
            v = v + rz[n, d].astype(F32)
        o[n, core, xx, yy] = v.astype(BF16)
        start(gather_copies(n))

    def do_gather(n):
        wait_all(15, g1r.at[n])
        gc_copy(n).start()

    br = (vcot[...].astype(F32) + dot(bpre[...], vup[...], ((1,), (1,)))).astype(BF16)
    bres[...] = br
    for m in range(M):
        y[m, 1:5] = br[m * 192 : (m + 1) * 192].reshape(PAIRS, 48, C)
    fill_stage(y, 1)
    do_core(0)
    do_core(1)
    for n in range(2):
        put(2 + n, dot(spread[:, n * 512 : (n + 1) * 512], bres[...], rows0))
        core_copy(2 + n).start()

    do_core(2)
    do_core(3)
    halo_y[0]()
    vline[...] = jnp.where(keep, dot(near, vselb[...]), 0.0)
    group = (lax.broadcasted_iota(jnp.int32, (8, K * 256), 1) // 32) % 8
    total = jnp.zeros((8, K * 256), F32)
    for r in range(A_TAPS):
        total = total + jnp.where(group == r, vline[r : r + 8], 0.0)
    lines[...] = total
    bands(lambda i, k: lines[i : i + 1, k * 256 : (k + 1) * 256], tap_b)

    for n in range(4):
        do_plane(n)

    vout[...] = (resid[...].astype(F32) + dot(hidden[...], vdown[...])).astype(BF16)
    halo_x[2]()
    halo_y[2]()
    for n in range(4):
        core_copy(n).wait_send()
        wait_all(15, s1s.at[n])
    for n in range(4):
        do_z(n)
    for n in range(4):
        wait_all(7, zs.at[n])
    halo_y[1]()
    stencil(tap_b, y, ys, spread)
    for m in range(M):
        at = slice(m * 192, (m + 1) * 192)
        acc = bres[at].astype(F32)
        for k in range(K):
            acc = acc + dot(
                spread[at, k * C : (k + 1) * C], vdisco[k * C : (k + 1) * C], ((1,), (1,))
            )
        vback[at] = acc.astype(BF16)

    for n in range(4):
        do_gather(n)

    for n in range(4):
        wait_all(15, g1s.at[n])
    for n in range(4):
        gc_copy(n).wait_recv()
        whole = o[n].astype(F32)
        if n == 0:
            down_out[...] = whole.reshape(FF, C)
        elif n == 1:
            up_out[:, :C] = whole[0].reshape(C, C)
            up_out[:, C:] = whole[1].reshape(C, C)
        else:
            disco_out[(n - 2) * 512 : (n - 1) * 512] = whole.reshape(512, C)
    for n in range(4):
        gc_copy(n).wait_send()


def finish(*refs):
    sem = refs[10]
    copies = [pltpu.make_async_copy(refs[n], refs[5 + n], sem.at[n]) for n in (2, 3, 4, 0, 1)]
    for c in copies:
        c.start()
    for c in copies:
        c.wait()


def per_device(fields, filters, lon_width, disco_weight, up_weight, down_weight, cotangent):
    flat = filters.transpose(1, 2, 3, 0).reshape(A_TAPS * B_TAPS, K, NLAT)
    sel_f, sel_b, perm, edge = [jnp.asarray(v) for v in constants()]
    vspec = pl.BlockSpec(memory_space=pltpu.VMEM)
    anyspec = pl.BlockSpec(memory_space=pl.ANY)
    dma = pltpu.SemaphoreType.DMA
    vm = pltpu.VMEM
    scratch = [
        vm((M, 6, OWN, C), BF16),
        vm((M, 6, OWN, C), BF16),
        vm((6, SIDES, C), BF16),
        vm((6, SIDES, C), BF16),
        vm((2, 2, PAIRS, 16, C), BF16),
        vm((TOK, C), BF16),
        vm((K * C, C), BF16),
        vm((C, FF), BF16),
        vm((FF, C), BF16),
        vm((A_TAPS * B_TAPS, K, NLAT), BF16),
        vm((NF, NLAT), F32),
        vm((NF, K * 256), BF16),
        vm((NF, K * 256), BF16),
        vm((2, 256, M * 256), BF16),
        vm((2 * PAIRS * 16, TOK), BF16),
        vm((16, K * 256), F32),
        vm((8, K * 256), F32),
        vm((2, PAIRS * 96, 256), BF16),
        vm((M, PAIRS, 192, 256), BF16),
        vm((M, PAIRS, 192, 256), BF16),
        vm((TOK, K * C), BF16),
        vm((TOK, FF), F32),
        vm((TOK, FF), F32),
        vm((TOK, FF), BF16),
        vm((TOK, FF), BF16),
        vm((TOK, C), BF16),
        vm((TOK, C), BF16),
        vm((4, 2, 4, 4, 16, C), BF16),
        vm((4, 4, 4, 16, C), BF16),
        vm((4, 4, 4, 16, C), BF16),
        vm((4, 15, 16, C), BF16),
        vm((4, 8, 16, C), BF16),
        vm((4, 2, 4, 4, 16, C), BF16),
        dma((10,)),
        dma((2, 8)),
        dma((2, 8)),
        dma((4,)),
        dma((4,)),
        dma((4,)),
        dma((4,)),
        dma((4,)),
        dma((4,)),
        dma((4,)),
        dma((4,)),
        dma((4,)),
        dma((4,)),
    ]
    results = (((TOK, C), BF16), ((TOK, C), BF16), ((K * C, C), F32), ((C, FF), F32), ((FF, C), F32))
    inner = pl.pallas_call(
        kernel,
        out_shape=[vm(*r) for r in results],
        in_specs=[pl.BlockSpec(memory_space=pltpu.SMEM)] + [pl.BlockSpec(memory_space=pltpu.HBM)] * 10,
        out_specs=[vspec] * 5,
        scratch_shapes=scratch,
        compiler_params=pltpu.CompilerParams(
            collective_id=0, has_side_effects=True, vmem_limit_bytes=60 * 2**20
        ),
    )(
        lon_width,
        fields.reshape(M, PAIRS, 48, C),
        cotangent.reshape(TOK, C),
        disco_weight.reshape(K * C, C),
        up_weight,
        down_weight,
        flat,
        sel_f,
        sel_b,
        perm,
        edge,
    )
    out, back, disco, up, down = pl.pallas_call(
        finish,
        out_shape=[jax.ShapeDtypeStruct(*r) for r in results],
        in_specs=[vspec] * 5,
        out_specs=[pl.BlockSpec(memory_space=pltpu.HBM)] * 5,
        scratch_shapes=[dma((5,))],
        compiler_params=pltpu.CompilerParams(vmem_limit_bytes=16 * 2**20),
    )(*[pltpu.with_memory_space_constraint(v, pltpu.VMEM) for v in inner])
    shape = fields.shape
    return out.reshape(shape), back.reshape(shape), disco.reshape(K, C, C), up, down


def solution(mesh):
    placed = (P(None, "lat", "lon", None), P(), P(), P(), P(), P(), P(None, "lat", "lon", None))
    return jax.shard_map(
        per_device,
        mesh=mesh,
        in_specs=placed,
        out_specs=(P(None, "lat", "lon", None), P(None, "lat", "lon", None), P(), P(), P()),
        check_vma=False,
    )
```

```python
import functools

import jax
import jax.numpy as jnp
import numpy as np
from jax import lax
from jax.experimental import pallas as pl
from jax.experimental.pallas import tpu as pltpu
from jax.sharding import PartitionSpec as P

GELU_SCALE = 0.7978845608028654
GELU_CUBE = 0.044715
MESH = pl.DeviceIdType.MESH
F32 = jnp.float32
BF16 = jnp.bfloat16

M, ROWS, CELLS, C, FF, K = 2, 8, 24, 256, 512, 4
NLAT = 64
A_TAPS, B_TAPS = 5, 9
PAIRS = ROWS // 2
TOK = M * ROWS * CELLS
OWN, SIDES = 48, 32
NK = 3 * (OWN + SIDES)
NF = A_TAPS * B_TAPS * 8
PLANE = sorted(
    [(dx, dy) for dx in range(4) for dy in range(4) if dx or dy],
    key=lambda t: (-min(t[0], 4 - t[0]) - min(t[1], 4 - t[1]), t),
)
RING = (4, 3, 5, 2, 6, 1, 7)


def constants():
    sel_f = np.zeros((NF, K * 256), np.float32)
    sel_b = np.zeros((NF, K * 256), np.float32)
    for a in range(A_TAPS):
        for b in range(B_TAPS):
            for k in range(K):
                s = (a * B_TAPS + b) * 8 + k
                sel_f[s, k * 256 + a * 32 + b] = 1
                sel_b[s, k * 256 + (4 - a) * 32 + 8 - b] = 1
    perm = np.zeros((2, 256, M * 256), np.float32)
    for i2 in range(2):
        for a in range(A_TAPS):
            p, r2 = divmod(i2 + a, 2)
            for jj in range(32):
                for m in range(M):
                    side = 3 * OWN + p * SIDES + m * 8 + r2 * 4
                    if jj < 4:
                        col = side + jj
                    elif jj < 28:
                        col = p * OWN + r2 * CELLS + jj - 4
                    else:
                        col = side + 16 + jj - 28
                    perm[i2, a * 32 + jj, m * 256 + col] = 1
    edge = np.zeros((2 * PAIRS * 16, TOK), np.float32)
    for side in range(2):
        for q in range(PAIRS):
            for m in range(M):
                for r2 in range(2):
                    for j in range(4):
                        cell = (CELLS - 4 + j) if side == 0 else j
                        token = ((m * PAIRS + q) * 2 + r2) * CELLS + cell
                        edge[(side * PAIRS + q) * 16 + m * 8 + r2 * 4 + j, token] = 1
    return [x.astype(jnp.bfloat16) for x in (sel_f, sel_b, perm, edge)]


def dot(a, b, dims=((1,), (0,))):
    return lax.dot_general(a, b, (dims, ((), ())), preferred_element_type=F32)


def kernel(
    lw, fields, cot, disco, up, down, filt, sel_f, sel_b, perm, edge,
    vout, vback, disco_out, up_out, down_out,
    x, y, xs, ys, stage, vcot, vdisco, vup, vdown, vfilt, filt8, vself, vselb, vperm, vedge,
    vline, lines, band, tap_f, tap_b, spread, pre, cd, hidden, bpre, resid, bres,
    g, rc, a1, r1, rz, o,
    lsem, hs, hr, cs, cr, s1s, s1r, zs, zr, g1s, g1r, gcs, gcr, vouch1, vouch2,
):
    lat, lon = lax.axis_index("lat"), lax.axis_index("lon")
    x_hi, yy = lat // 4, lat % 4
    zz, x_lo, core = lon // 4, (lon // 2) % 2, lon % 2
    xx = x_hi * 2 + x_lo

    def at_xy(dx, dy):
        v = (xx + dx) % 4
        return ((v // 2) * 4 + (yy + dy) % 4, zz * 4 + (v % 2) * 2 + core)

    def at_z(d):
        return (lat, ((zz + d) % 8) * 4 + x_lo * 2 + core)

    pair = (lat, zz * 4 + x_lo * 2 + (1 - core))
    right, left = (lon + 1) % 32, (lon + 31) % 32
    has_up, has_down = lat > 0, lat < 7

    loads = [
        pltpu.make_async_copy(fields, x.at[:, 1:5], lsem.at[0]),
        pltpu.make_async_copy(edge, vedge, lsem.at[1]),
        pltpu.make_async_copy(filt, vfilt, lsem.at[2]),
        pltpu.make_async_copy(sel_f, vself, lsem.at[3]),
        pltpu.make_async_copy(perm, vperm, lsem.at[4]),
        pltpu.make_async_copy(cot, vcot, lsem.at[5]),
        pltpu.make_async_copy(down, vdown, lsem.at[6]),
        pltpu.make_async_copy(disco, vdisco, lsem.at[7]),
        pltpu.make_async_copy(up, vup, lsem.at[8]),
        pltpu.make_async_copy(sel_b, vselb, lsem.at[9]),
    ]
    for c in loads:
        c.start()

    barrier = pltpu.get_barrier_semaphore()

    def hello(dev):
        pl.semaphore_signal(barrier, inc=1, device_id=dev, device_id_type=MESH)

    hello((lat, right))
    hello((lat, left))

    @pl.when(has_up)
    def _():
        for v in (left, lon, right):
            hello((lat - 1, v))

    @pl.when(has_down)
    def _():
        for v in (left, lon, right):
            hello((lat + 1, v))

    near_chips = [at_xy(dx, dy) for dx, dy in PLANE if dx != 2 and dy != 2] + [at_z(1), at_z(7)]
    for dev in near_chips:
        hello(dev)

    def clear(n):
        for buf, sides in ((x, xs), (y, ys)):
            buf[:, n] = jnp.zeros((M, OWN, C), BF16)
            sides[n] = jnp.zeros((SIDES, C), BF16)

    @pl.when(lat == 0)
    def _():
        clear(0)

    @pl.when(lat == 7)
    def _():
        clear(5)

    def rdma(src, dst, ss, rs, dev):
        return pltpu.make_async_remote_copy(
            src_ref=src, dst_ref=dst, send_sem=ss, recv_sem=rs, device_id=dev, device_id_type=MESH
        )

    def halo(buf, sides, ph):
        st = stage.at[ph]

        def lon_copies():
            return [
                rdma(st.at[0], sides.at[1:5, 0:16], hs.at[ph, 0], hr.at[ph, 0], (lat, right)),
                rdma(st.at[1], sides.at[1:5, 16:32], hs.at[ph, 1], hr.at[ph, 1], (lat, left)),
            ]

        def to_down():
            return [
                rdma(buf.at[:, 4], buf.at[:, 0], hs.at[ph, 2], hr.at[ph, 2], (lat + 1, lon)),
                rdma(st.at[0, 3], sides.at[0, 0:16], hs.at[ph, 3], hr.at[ph, 3], (lat + 1, right)),
                rdma(st.at[1, 3], sides.at[0, 16:32], hs.at[ph, 4], hr.at[ph, 4], (lat + 1, left)),
            ]

        def to_up():
            return [
                rdma(buf.at[:, 1], buf.at[:, 5], hs.at[ph, 5], hr.at[ph, 5], (lat - 1, lon)),
                rdma(st.at[0, 0], sides.at[5, 0:16], hs.at[ph, 6], hr.at[ph, 6], (lat - 1, right)),
                rdma(st.at[1, 0], sides.at[5, 16:32], hs.at[ph, 7], hr.at[ph, 7], (lat - 1, left)),
            ]

        def start():
            @pl.when(has_down)
            def _():
                for c in to_down():
                    c.start()

            @pl.when(has_up)
            def _():
                for c in to_up():
                    c.start()

            for c in lon_copies():
                c.start()

        def recv():
            for c in lon_copies():
                c.wait_recv()

            @pl.when(has_up)
            def _():
                for c in to_down():
                    c.wait_recv()

            @pl.when(has_down)
            def _():
                for c in to_up():
                    c.wait_recv()

        def sent():
            for c in lon_copies():
                c.wait_send()

            @pl.when(has_down)
            def _():
                for c in to_down():
                    c.wait_send()

            @pl.when(has_up)
            def _():
                for c in to_up():
                    c.wait_send()

        return start, recv, sent

    halo_x = halo(x, xs, 0)
    halo_y = halo(y, ys, 1)

    def own(buf, m):
        return buf[m, 1:5].reshape(ROWS * CELLS, C)

    def fill_stage(buf, ph):
        e = dot(vedge[...], buf[:, 1:5].reshape(TOK, C)).astype(BF16)
        stage[ph] = e.reshape(2, PAIRS, 16, C)

    loads[0].wait()
    loads[1].wait()
    fill_stage(x, 0)
    pl.semaphore_wait(
        barrier, 12 + 3 * has_up.astype(jnp.int32) + 3 * has_down.astype(jnp.int32)
    )
    halo_x[0]()

    def vouch(sem, devs):
        for dev in devs:
            pl.semaphore_signal(sem, inc=1, device_id=dev, device_id_type=MESH)

    vouch(vouch1, near_chips)

    loads[2].wait()
    filt8[...] = jnp.zeros_like(filt8)
    for n in range(A_TAPS * B_TAPS):
        filt8[n * 8 : n * 8 + K] = vfilt[n].astype(F32)
    first = lat * ROWS - 2
    row_sel = (
        lax.broadcasted_iota(jnp.int32, (16, NLAT), 1)
        == lax.broadcasted_iota(jnp.int32, (16, NLAT), 0) + first
    )
    near = dot(jnp.where(row_sel, 1.0, 0.0).astype(BF16), filt8[...].astype(BF16), ((1,), (1,))).astype(BF16)
    line_row = lax.broadcasted_iota(jnp.int32, (16, K * 256), 0)
    reach = jnp.zeros((16, K * 256), jnp.int32)
    for r in range(12):
        reach = jnp.where(line_row == r, lw[jnp.clip(first + r, 0, NLAT - 1)], reach)
    lane = lax.broadcasted_iota(jnp.int32, (16, K * 256), 1)
    keep = jnp.abs((lane & 31) - 4) <= reach

    def bands(get_line, tap):
        for i in range(ROWS):
            q, i2 = divmod(i, 2)
            parts = []
            for k in range(K):
                line = jnp.broadcast_to(get_line(i, k), (CELLS, 256))
                parts.append(
                    jnp.concatenate(
                        [
                            pltpu.roll(line[:, h * 128 : (h + 1) * 128], 0, 1, stride=1, stride_axis=0)
                            for h in range(2)
                        ],
                        axis=1,
                    )
                )
            band[i2, q * 96 : (q + 1) * 96] = jnp.concatenate(parts, axis=0).astype(BF16)
        res = [dot(band[i2], vperm[i2]) for i2 in range(2)]
        for q in range(PAIRS):
            for k in range(K):
                at = q * 96 + k * CELLS
                both = jnp.concatenate([res[0][at : at + CELLS], res[1][at : at + CELLS]], axis=0)
                for m in range(M):
                    tap[m, q, k * 48 : (k + 1) * 48] = both[:, m * 256 : (m + 1) * 256].astype(BF16)

    loads[3].wait()
    loads[4].wait()
    vline[...] = jnp.where(keep, dot(near, vself[...]), 0.0)
    bands(lambda i, k: vline[i + 2 : i + 3, k * 256 : (k + 1) * 256], tap_f)

    loads[5].wait()
    loads[6].wait()
    cd[...] = dot(vcot[...], vdown[...], ((1,), (1,)))
    loads[9].wait()
    loads[7].wait()
    loads[8].wait()

    def stencil(tap, buf, sides, dst):
        for q in range(PAIRS):
            for m in range(M):
                window = jnp.concatenate(
                    [buf[m, q : q + 3].reshape(3 * OWN, C), sides[q : q + 3].reshape(3 * SIDES, C)], axis=0
                )
                res = dot(tap[m, q][:, :NK], window).astype(BF16)
                for k in range(K):
                    at = m * 192 + q * 48
                    dst[at : at + 48, k * C : (k + 1) * C] = res[k * 48 : (k + 1) * 48]

    halo_x[1]()
    stencil(tap_f, x, xs, spread)

    for m in range(M):
        mixed = dot(spread[m * 192 : (m + 1) * 192], vdisco[...])
        resid[m * 192 : (m + 1) * 192] = (own(x, m).astype(F32) + mixed).astype(BF16)
    pre[...] = dot(resid[...], vup[...])

    @pl.loop(0, TOK // 16)
    def _(n):
        at = pl.ds(pl.multiple_of(n * 16, 16), 16)
        p = pre[at]
        pp = p * p
        t = jnp.tanh(GELU_SCALE * p * (1.0 + GELU_CUBE * pp))
        h = 0.5 * (1.0 + t)
        hidden[at] = (p * h).astype(BF16)
        slope = h + 0.5 * p * (1.0 - t * t) * GELU_SCALE * (1.0 + 3.0 * GELU_CUBE * pp)
        bpre[at] = (cd[at] * slope).astype(BF16)

    rows0 = ((0,), (0,))

    def put(n, value):
        g[n] = value.astype(BF16).reshape(2, 4, 4, 16, C)

    def core_copy(n):
        return rdma(g.at[n, 1 - core], rc.at[n], cs.at[n], cr.at[n], pair)

    put(0, dot(hidden[...], vcot[...], rows0))
    core_copy(0).start()
    gu = dot(resid[...], bpre[...], rows0)
    put(1, jnp.concatenate([gu[:, :C], gu[:, C:]], axis=0))
    core_copy(1).start()

    def plane_copies(n):
        return [
            rdma(
                a1.at[n, (xx + dx) % 4, (yy + dy) % 4], r1.at[n, i], s1s.at[n], s1r.at[n],
                at_xy(dx, dy),
            )
            for i, (dx, dy) in enumerate(PLANE)
        ]

    def z_copies(n):
        ref = rz.at[n, zz]
        return [rdma(ref, ref, zs.at[n], zr.at[n], at_z(d)) for d in RING]

    def gather_copies(n):
        ref = o.at[n, core, xx, yy]
        return [
            rdma(ref, ref, g1s.at[n], g1r.at[n], at_xy(dx, dy))
            for dx, dy in PLANE
        ]

    def gc_copy(n):
        ref = o.at[n, core]
        return rdma(ref, ref, gcs.at[n], gcr.at[n], pair)

    def start(copies):
        for c in copies:
            c.start()

    def wait_all(blocks, sem):
        ref = r1.at[0, 0:blocks]
        pltpu.make_async_copy(ref, ref, sem).wait()

    def do_core(n):
        core_copy(n).wait_recv()
        a1[n] = (g[n, core].astype(F32) + rc[n].astype(F32)).astype(BF16)
        start(plane_copies(n))

    def do_plane(n):
        wait_all(15, s1r.at[n])
        v = a1[n, xx, yy].astype(F32)
        for d in range(15):
            v = v + r1[n, d].astype(F32)
        rz[n, zz] = v.astype(BF16)
        start(z_copies(n))

    def do_z(n):
        wait_all(7, zr.at[n])
        v = rz[n, 0].astype(F32)
        for d in range(1, 8):
            v = v + rz[n, d].astype(F32)
        o[n, core, xx, yy] = v.astype(BF16)
        start(gather_copies(n))

    def do_gather(n):
        wait_all(15, g1r.at[n])
        gc_copy(n).start()

    br = (vcot[...].astype(F32) + dot(bpre[...], vup[...], ((1,), (1,)))).astype(BF16)
    bres[...] = br
    for m in range(M):
        y[m, 1:5] = br[m * 192 : (m + 1) * 192].reshape(PAIRS, 48, C)
    fill_stage(y, 1)
    pl.semaphore_wait(vouch1, 10)
    vouch(vouch2, [at_z(2), at_z(6)])
    do_core(0)
    do_core(1)
    for n in range(2):
        put(2 + n, dot(spread[:, n * 512 : (n + 1) * 512], bres[...], rows0))
        core_copy(2 + n).start()

    do_core(2)
    do_core(3)
    halo_y[0]()
    vline[...] = jnp.where(keep, dot(near, vselb[...]), 0.0)
    group = (lax.broadcasted_iota(jnp.int32, (8, K * 256), 1) // 32) % 8
    total = jnp.zeros((8, K * 256), F32)
    for r in range(A_TAPS):
        total = total + jnp.where(group == r, vline[r : r + 8], 0.0)
    lines[...] = total
    bands(lambda i, k: lines[i : i + 1, k * 256 : (k + 1) * 256], tap_b)

    pl.semaphore_wait(vouch2, 2)
    for n in range(4):
        do_plane(n)

    vout[...] = (resid[...].astype(F32) + dot(hidden[...], vdown[...])).astype(BF16)
    halo_x[2]()
    halo_y[2]()
    for n in range(4):
        core_copy(n).wait_send()
        wait_all(15, s1s.at[n])
    for n in range(4):
        do_z(n)
    for n in range(4):
        wait_all(7, zs.at[n])
    halo_y[1]()
    stencil(tap_b, y, ys, spread)
    for m in range(M):
        at = slice(m * 192, (m + 1) * 192)
        acc = bres[at].astype(F32)
        for k in range(K):
            acc = acc + dot(
                spread[at, k * C : (k + 1) * C], vdisco[k * C : (k + 1) * C], ((1,), (1,))
            )
        vback[at] = acc.astype(BF16)

    for n in range(4):
        do_gather(n)

    for n in range(4):
        wait_all(15, g1s.at[n])
    for n in range(4):
        gc_copy(n).wait_recv()
        whole = o[n].astype(F32)
        if n == 0:
            down_out[...] = whole.reshape(FF, C)
        elif n == 1:
            up_out[:, :C] = whole[0].reshape(C, C)
            up_out[:, C:] = whole[1].reshape(C, C)
        else:
            disco_out[(n - 2) * 512 : (n - 1) * 512] = whole.reshape(512, C)
    for n in range(4):
        gc_copy(n).wait_send()


def finish(*refs):
    sem = refs[10]
    copies = [pltpu.make_async_copy(refs[n], refs[5 + n], sem.at[n]) for n in (2, 3, 4, 0, 1)]
    for c in copies:
        c.start()
    for c in copies:
        c.wait()


def per_device(fields, filters, lon_width, disco_weight, up_weight, down_weight, cotangent):
    flat = filters.transpose(1, 2, 3, 0).reshape(A_TAPS * B_TAPS, K, NLAT)
    sel_f, sel_b, perm, edge = [jnp.asarray(v) for v in constants()]
    vspec = pl.BlockSpec(memory_space=pltpu.VMEM)
    anyspec = pl.BlockSpec(memory_space=pl.ANY)
    dma = pltpu.SemaphoreType.DMA
    vm = pltpu.VMEM
    scratch = [
        vm((M, 6, OWN, C), BF16),
        vm((M, 6, OWN, C), BF16),
        vm((6, SIDES, C), BF16),
        vm((6, SIDES, C), BF16),
        vm((2, 2, PAIRS, 16, C), BF16),
        vm((TOK, C), BF16),
        vm((K * C, C), BF16),
        vm((C, FF), BF16),
        vm((FF, C), BF16),
        vm((A_TAPS * B_TAPS, K, NLAT), BF16),
        vm((NF, NLAT), F32),
        vm((NF, K * 256), BF16),
        vm((NF, K * 256), BF16),
        vm((2, 256, M * 256), BF16),
        vm((2 * PAIRS * 16, TOK), BF16),
        vm((16, K * 256), F32),
        vm((8, K * 256), F32),
        vm((2, PAIRS * 96, 256), BF16),
        vm((M, PAIRS, 192, 256), BF16),
        vm((M, PAIRS, 192, 256), BF16),
        vm((TOK, K * C), BF16),
        vm((TOK, FF), F32),
        vm((TOK, FF), F32),
        vm((TOK, FF), BF16),
        vm((TOK, FF), BF16),
        vm((TOK, C), BF16),
        vm((TOK, C), BF16),
        vm((4, 2, 4, 4, 16, C), BF16),
        vm((4, 4, 4, 16, C), BF16),
        vm((4, 4, 4, 16, C), BF16),
        vm((4, 15, 16, C), BF16),
        vm((4, 8, 16, C), BF16),
        vm((4, 2, 4, 4, 16, C), BF16),
        dma((10,)),
        dma((2, 8)),
        dma((2, 8)),
        dma((4,)),
        dma((4,)),
        dma((4,)),
        dma((4,)),
        dma((4,)),
        dma((4,)),
        dma((4,)),
        dma((4,)),
        dma((4,)),
        dma((4,)),
        pltpu.SemaphoreType.REGULAR,
        pltpu.SemaphoreType.REGULAR,
    ]
    results = (((TOK, C), BF16), ((TOK, C), BF16), ((K * C, C), F32), ((C, FF), F32), ((FF, C), F32))
    inner = pl.pallas_call(
        kernel,
        out_shape=[vm(*r) for r in results],
        in_specs=[pl.BlockSpec(memory_space=pltpu.SMEM)] + [pl.BlockSpec(memory_space=pltpu.HBM)] * 10,
        out_specs=[vspec] * 5,
        scratch_shapes=scratch,
        compiler_params=pltpu.CompilerParams(
            collective_id=0, has_side_effects=True, vmem_limit_bytes=60 * 2**20
        ),
    )(
        lon_width,
        fields.reshape(M, PAIRS, 48, C),
        cotangent.reshape(TOK, C),
        disco_weight.reshape(K * C, C),
        up_weight,
        down_weight,
        flat,
        sel_f,
        sel_b,
        perm,
        edge,
    )
    out, back, disco, up, down = pl.pallas_call(
        finish,
        out_shape=[jax.ShapeDtypeStruct(*r) for r in results],
        in_specs=[vspec] * 5,
        out_specs=[pl.BlockSpec(memory_space=pltpu.HBM)] * 5,
        scratch_shapes=[dma((5,))],
        compiler_params=pltpu.CompilerParams(vmem_limit_bytes=16 * 2**20),
    )(*[pltpu.with_memory_space_constraint(v, pltpu.VMEM) for v in inner])
    shape = fields.shape
    return out.reshape(shape), back.reshape(shape), disco.reshape(K, C, C), up, down


def solution(mesh):
    placed = (P(None, "lat", "lon", None), P(), P(), P(), P(), P(), P(None, "lat", "lon", None))
    return jax.shard_map(
        per_device,
        mesh=mesh,
        in_specs=placed,
        out_specs=(P(None, "lat", "lon", None), P(None, "lat", "lon", None), P(), P(), P()),
        check_vma=False,
    )
```

```python
import functools

import jax
import jax.numpy as jnp
import numpy as np
from jax import lax
from jax.experimental import pallas as pl
from jax.experimental.pallas import tpu as pltpu
from jax.sharding import PartitionSpec as P

GELU_SCALE = 0.7978845608028654
GELU_CUBE = 0.044715
MESH = pl.DeviceIdType.MESH
F32 = jnp.float32
BF16 = jnp.bfloat16

M, ROWS, CELLS, C, FF, K = 2, 8, 24, 256, 512, 4
NLAT = 64
A_TAPS, B_TAPS = 5, 9
PAIRS = ROWS // 2
TOK = M * ROWS * CELLS
OWN, SIDES = 48, 32
NK = 3 * (OWN + SIDES)
NF = A_TAPS * B_TAPS * 8
PLANE = sorted(
    [(dx, dy) for dx in range(4) for dy in range(4) if dx or dy],
    key=lambda t: (-min(t[0], 4 - t[0]) - min(t[1], 4 - t[1]), t),
)
RING = (4, 3, 5, 2, 6, 1, 7)


def constants():
    sel_f = np.zeros((NF, K * 256), np.float32)
    sel_b = np.zeros((NF, K * 256), np.float32)
    for a in range(A_TAPS):
        for b in range(B_TAPS):
            for k in range(K):
                s = (a * B_TAPS + b) * 8 + k
                sel_f[s, k * 256 + a * 32 + b] = 1
                sel_b[s, k * 256 + (4 - a) * 32 + 8 - b] = 1
    perm = np.zeros((2, 256, M * 256), np.float32)
    for i2 in range(2):
        for a in range(A_TAPS):
            p, r2 = divmod(i2 + a, 2)
            for jj in range(32):
                for m in range(M):
                    side = 3 * OWN + p * SIDES + m * 8 + r2 * 4
                    if jj < 4:
                        col = side + jj
                    elif jj < 28:
                        col = p * OWN + r2 * CELLS + jj - 4
                    else:
                        col = side + 16 + jj - 28
                    perm[i2, a * 32 + jj, m * 256 + col] = 1
    edge = np.zeros((2 * PAIRS * 16, TOK), np.float32)
    for side in range(2):
        for q in range(PAIRS):
            for m in range(M):
                for r2 in range(2):
                    for j in range(4):
                        cell = (CELLS - 4 + j) if side == 0 else j
                        token = ((m * PAIRS + q) * 2 + r2) * CELLS + cell
                        edge[(side * PAIRS + q) * 16 + m * 8 + r2 * 4 + j, token] = 1
    return [x.astype(jnp.bfloat16) for x in (sel_f, sel_b, perm, edge)]


def dot(a, b, dims=((1,), (0,))):
    return lax.dot_general(a, b, (dims, ((), ())), preferred_element_type=F32)


def kernel(
    width, fields, cot, disco, up, down, filt, sel_f, sel_b, perm, edge,
    vout, vback, disco_out, up_out, down_out,
    lw, x, y, xs, ys, stage, vcot, vdisco, vup, vdown, vfilt, filt8, vself, vselb, vperm, vedge,
    vline, lines, band, tap_f, tap_b, spread, pre, cd, hidden, bpre, resid, bres,
    g, rc, a1, r1, rz, o,
    lsem, hs, hr, cs, cr, s1s, s1r, zs, zr, g1s, g1r, gcs, gcr, vouch1, vouch2,
):
    lat, lon = lax.axis_index("lat"), lax.axis_index("lon")
    x_hi, yy = lat // 4, lat % 4
    zz, x_lo, core = lon // 4, (lon // 2) % 2, lon % 2
    xx = x_hi * 2 + x_lo

    def at_xy(dx, dy):
        v = (xx + dx) % 4
        return ((v // 2) * 4 + (yy + dy) % 4, zz * 4 + (v % 2) * 2 + core)

    def at_z(d):
        return (lat, ((zz + d) % 8) * 4 + x_lo * 2 + core)

    pair = (lat, zz * 4 + x_lo * 2 + (1 - core))
    right, left = (lon + 1) % 32, (lon + 31) % 32
    has_up, has_down = lat > 0, lat < 7

    loads = [
        pltpu.make_async_copy(fields, x.at[:, 1:5], lsem.at[0]),
        pltpu.make_async_copy(edge, vedge, lsem.at[1]),
        pltpu.make_async_copy(filt, vfilt, lsem.at[2]),
        pltpu.make_async_copy(sel_f, vself, lsem.at[3]),
        pltpu.make_async_copy(perm, vperm, lsem.at[4]),
        pltpu.make_async_copy(cot, vcot, lsem.at[5]),
        pltpu.make_async_copy(down, vdown, lsem.at[6]),
        pltpu.make_async_copy(disco, vdisco, lsem.at[7]),
        pltpu.make_async_copy(up, vup, lsem.at[8]),
        pltpu.make_async_copy(sel_b, vselb, lsem.at[9]),
        pltpu.make_async_copy(width, lw, lsem.at[10]),
    ]
    loads[0].start()
    loads[1].start()

    barrier = pltpu.get_barrier_semaphore()

    def hello(dev):
        pl.semaphore_signal(barrier, inc=1, device_id=dev, device_id_type=MESH)

    hello((lat, right))
    hello((lat, left))

    @pl.when(has_up)
    def _():
        for v in (left, lon, right):
            hello((lat - 1, v))

    @pl.when(has_down)
    def _():
        for v in (left, lon, right):
            hello((lat + 1, v))

    near_chips = [at_xy(dx, dy) for dx, dy in PLANE if dx != 2 and dy != 2] + [at_z(1), at_z(7)]
    for dev in near_chips:
        hello(dev)

    for c in loads[2:]:
        c.start()

    def clear(n):
        for buf, sides in ((x, xs), (y, ys)):
            buf[:, n] = jnp.zeros((M, OWN, C), BF16)
            sides[n] = jnp.zeros((SIDES, C), BF16)

    @pl.when(lat == 0)
    def _():
        clear(0)

    @pl.when(lat == 7)
    def _():
        clear(5)

    def rdma(src, dst, ss, rs, dev):
        return pltpu.make_async_remote_copy(
            src_ref=src, dst_ref=dst, send_sem=ss, recv_sem=rs, device_id=dev, device_id_type=MESH
        )

    def halo(buf, sides, ph):
        st = stage.at[ph]

        def lon_copies():
            return [
                rdma(st.at[0], sides.at[1:5, 0:16], hs.at[ph, 0], hr.at[ph, 0], (lat, right)),
                rdma(st.at[1], sides.at[1:5, 16:32], hs.at[ph, 1], hr.at[ph, 1], (lat, left)),
            ]

        def to_down():
            return [
                rdma(buf.at[:, 4], buf.at[:, 0], hs.at[ph, 2], hr.at[ph, 2], (lat + 1, lon)),
                rdma(st.at[0, 3], sides.at[0, 0:16], hs.at[ph, 3], hr.at[ph, 3], (lat + 1, right)),
                rdma(st.at[1, 3], sides.at[0, 16:32], hs.at[ph, 4], hr.at[ph, 4], (lat + 1, left)),
            ]

        def to_up():
            return [
                rdma(buf.at[:, 1], buf.at[:, 5], hs.at[ph, 5], hr.at[ph, 5], (lat - 1, lon)),
                rdma(st.at[0, 0], sides.at[5, 0:16], hs.at[ph, 6], hr.at[ph, 6], (lat - 1, right)),
                rdma(st.at[1, 0], sides.at[5, 16:32], hs.at[ph, 7], hr.at[ph, 7], (lat - 1, left)),
            ]

        def start():
            @pl.when(has_down)
            def _():
                for c in to_down():
                    c.start()

            @pl.when(has_up)
            def _():
                for c in to_up():
                    c.start()

            for c in lon_copies():
                c.start()

        def recv():
            for c in lon_copies():
                c.wait_recv()

            @pl.when(has_up)
            def _():
                for c in to_down():
                    c.wait_recv()

            @pl.when(has_down)
            def _():
                for c in to_up():
                    c.wait_recv()

        def sent():
            for c in lon_copies():
                c.wait_send()

            @pl.when(has_down)
            def _():
                for c in to_down():
                    c.wait_send()

            @pl.when(has_up)
            def _():
                for c in to_up():
                    c.wait_send()

        return start, recv, sent

    halo_x = halo(x, xs, 0)
    halo_y = halo(y, ys, 1)

    def own(buf, m):
        return buf[m, 1:5].reshape(ROWS * CELLS, C)

    def fill_stage(buf, ph):
        e = dot(vedge[...], buf[:, 1:5].reshape(TOK, C)).astype(BF16)
        stage[ph] = e.reshape(2, PAIRS, 16, C)

    loads[0].wait()
    loads[1].wait()
    fill_stage(x, 0)
    pl.semaphore_wait(
        barrier, 12 + 3 * has_up.astype(jnp.int32) + 3 * has_down.astype(jnp.int32)
    )
    halo_x[0]()

    def vouch(sem, devs):
        for dev in devs:
            pl.semaphore_signal(sem, inc=1, device_id=dev, device_id_type=MESH)

    vouch(vouch1, near_chips)

    loads[2].wait()
    loads[10].wait()
    filt8[...] = jnp.zeros_like(filt8)
    for n in range(A_TAPS * B_TAPS):
        filt8[n * 8 : n * 8 + K] = vfilt[n].astype(F32)
    first = lat * ROWS - 2
    row_sel = (
        lax.broadcasted_iota(jnp.int32, (16, NLAT), 1)
        == lax.broadcasted_iota(jnp.int32, (16, NLAT), 0) + first
    )
    near = dot(jnp.where(row_sel, 1.0, 0.0).astype(BF16), filt8[...].astype(BF16), ((1,), (1,))).astype(BF16)
    line_row = lax.broadcasted_iota(jnp.int32, (16, K * 256), 0)
    reach = jnp.zeros((16, K * 256), jnp.int32)
    for r in range(12):
        reach = jnp.where(line_row == r, lw[jnp.clip(first + r, 0, NLAT - 1)], reach)
    lane = lax.broadcasted_iota(jnp.int32, (16, K * 256), 1)
    keep = jnp.abs((lane & 31) - 4) <= reach

    def bands(get_line, tap):
        for i in range(ROWS):
            q, i2 = divmod(i, 2)
            parts = []
            for k in range(K):
                line = jnp.broadcast_to(get_line(i, k), (CELLS, 256))
                parts.append(
                    jnp.concatenate(
                        [
                            pltpu.roll(line[:, h * 128 : (h + 1) * 128], 0, 1, stride=1, stride_axis=0)
                            for h in range(2)
                        ],
                        axis=1,
                    )
                )
            band[i2, q * 96 : (q + 1) * 96] = jnp.concatenate(parts, axis=0).astype(BF16)
        res = [dot(band[i2], vperm[i2]) for i2 in range(2)]
        for q in range(PAIRS):
            for k in range(K):
                at = q * 96 + k * CELLS
                both = jnp.concatenate([res[0][at : at + CELLS], res[1][at : at + CELLS]], axis=0)
                for m in range(M):
                    tap[m, q, k * 48 : (k + 1) * 48] = both[:, m * 256 : (m + 1) * 256].astype(BF16)

    loads[3].wait()
    loads[4].wait()
    vline[...] = jnp.where(keep, dot(near, vself[...]), 0.0)
    bands(lambda i, k: vline[i + 2 : i + 3, k * 256 : (k + 1) * 256], tap_f)

    loads[5].wait()
    loads[6].wait()
    cd[...] = dot(vcot[...], vdown[...], ((1,), (1,)))
    loads[9].wait()
    loads[7].wait()
    loads[8].wait()

    def stencil(tap, buf, sides, dst):
        for q in range(PAIRS):
            for m in range(M):
                window = jnp.concatenate(
                    [buf[m, q : q + 3].reshape(3 * OWN, C), sides[q : q + 3].reshape(3 * SIDES, C)], axis=0
                )
                res = dot(tap[m, q][:, :NK], window).astype(BF16)
                for k in range(K):
                    at = m * 192 + q * 48
                    dst[at : at + 48, k * C : (k + 1) * C] = res[k * 48 : (k + 1) * 48]

    halo_x[1]()
    stencil(tap_f, x, xs, spread)

    for m in range(M):
        mixed = dot(spread[m * 192 : (m + 1) * 192], vdisco[...])
        resid[m * 192 : (m + 1) * 192] = (own(x, m).astype(F32) + mixed).astype(BF16)
    pre[...] = dot(resid[...], vup[...])

    @pl.loop(0, TOK // 16)
    def _(n):
        at = pl.ds(pl.multiple_of(n * 16, 16), 16)
        p = pre[at]
        pp = p * p
        t = jnp.tanh(GELU_SCALE * p * (1.0 + GELU_CUBE * pp))
        h = 0.5 * (1.0 + t)
        hidden[at] = (p * h).astype(BF16)
        slope = h + 0.5 * p * (1.0 - t * t) * GELU_SCALE * (1.0 + 3.0 * GELU_CUBE * pp)
        bpre[at] = (cd[at] * slope).astype(BF16)

    rows0 = ((0,), (0,))

    def put(n, value):
        g[n] = value.astype(BF16).reshape(2, 4, 4, 16, C)

    def core_copy(n):
        return rdma(g.at[n, 1 - core], rc.at[n], cs.at[n], cr.at[n], pair)

    put(0, dot(hidden[...], vcot[...], rows0))
    core_copy(0).start()
    gu = dot(resid[...], bpre[...], rows0)
    put(1, jnp.concatenate([gu[:, :C], gu[:, C:]], axis=0))
    core_copy(1).start()

    def plane_copies(n):
        return [
            rdma(
                a1.at[n, (xx + dx) % 4, (yy + dy) % 4], r1.at[n, i], s1s.at[n], s1r.at[n],
                at_xy(dx, dy),
            )
            for i, (dx, dy) in enumerate(PLANE)
        ]

    def z_copies(n):
        ref = rz.at[n, zz]
        return [rdma(ref, ref, zs.at[n], zr.at[n], at_z(d)) for d in RING]

    def gather_copies(n):
        ref = o.at[n, core, xx, yy]
        return [
            rdma(ref, ref, g1s.at[n], g1r.at[n], at_xy(dx, dy))
            for dx, dy in PLANE
        ]

    def gc_copy(n):
        ref = o.at[n, core]
        return rdma(ref, ref, gcs.at[n], gcr.at[n], pair)

    def start(copies):
        for c in copies:
            c.start()

    def wait_all(blocks, sem):
        ref = r1.at[0, 0:blocks]
        pltpu.make_async_copy(ref, ref, sem).wait()

    def do_core(n):
        core_copy(n).wait_recv()
        a1[n] = (g[n, core].astype(F32) + rc[n].astype(F32)).astype(BF16)
        start(plane_copies(n))

    def do_plane(n):
        wait_all(15, s1r.at[n])
        v = a1[n, xx, yy].astype(F32)
        for d in range(15):
            v = v + r1[n, d].astype(F32)
        rz[n, zz] = v.astype(BF16)
        start(z_copies(n))

    def do_z(n):
        wait_all(7, zr.at[n])
        v = rz[n, 0].astype(F32)
        for d in range(1, 8):
            v = v + rz[n, d].astype(F32)
        o[n, core, xx, yy] = v.astype(BF16)
        start(gather_copies(n))

    def do_gather(n):
        wait_all(15, g1r.at[n])
        gc_copy(n).start()

    br = (vcot[...].astype(F32) + dot(bpre[...], vup[...], ((1,), (1,)))).astype(BF16)
    bres[...] = br
    for m in range(M):
        y[m, 1:5] = br[m * 192 : (m + 1) * 192].reshape(PAIRS, 48, C)
    fill_stage(y, 1)
    pl.semaphore_wait(vouch1, 10)
    vouch(vouch2, [at_z(2), at_z(6)])
    do_core(0)
    do_core(1)
    for n in range(2):
        put(2 + n, dot(spread[:, n * 512 : (n + 1) * 512], bres[...], rows0))
        core_copy(2 + n).start()

    do_core(2)
    do_core(3)
    halo_y[0]()
    vline[...] = jnp.where(keep, dot(near, vselb[...]), 0.0)
    group = (lax.broadcasted_iota(jnp.int32, (8, K * 256), 1) // 32) % 8
    total = jnp.zeros((8, K * 256), F32)
    for r in range(A_TAPS):
        total = total + jnp.where(group == r, vline[r : r + 8], 0.0)
    lines[...] = total
    bands(lambda i, k: lines[i : i + 1, k * 256 : (k + 1) * 256], tap_b)

    pl.semaphore_wait(vouch2, 2)
    for n in range(4):
        do_plane(n)

    vout[...] = (resid[...].astype(F32) + dot(hidden[...], vdown[...])).astype(BF16)
    halo_x[2]()
    halo_y[2]()
    for n in range(4):
        core_copy(n).wait_send()
        wait_all(15, s1s.at[n])
    for n in range(4):
        do_z(n)
    for n in range(4):
        wait_all(7, zs.at[n])
    halo_y[1]()
    stencil(tap_b, y, ys, spread)
    for m in range(M):
        at = slice(m * 192, (m + 1) * 192)
        acc = bres[at].astype(F32)
        for k in range(K):
            acc = acc + dot(
                spread[at, k * C : (k + 1) * C], vdisco[k * C : (k + 1) * C], ((1,), (1,))
            )
        vback[at] = acc.astype(BF16)

    for n in range(4):
        do_gather(n)

    for n in range(4):
        wait_all(15, g1s.at[n])
    for n in range(4):
        gc_copy(n).wait_recv()
        whole = o[n].astype(F32)
        if n == 0:
            down_out[...] = whole.reshape(FF, C)
        elif n == 1:
            up_out[:, :C] = whole[0].reshape(C, C)
            up_out[:, C:] = whole[1].reshape(C, C)
        else:
            disco_out[(n - 2) * 512 : (n - 1) * 512] = whole.reshape(512, C)
    for n in range(4):
        gc_copy(n).wait_send()


def finish(*refs):
    sem = refs[10]
    copies = [pltpu.make_async_copy(refs[n], refs[5 + n], sem.at[n]) for n in (2, 3, 4, 0, 1)]
    for c in copies:
        c.start()
    for c in copies:
        c.wait()


def per_device(fields, filters, lon_width, disco_weight, up_weight, down_weight, cotangent):
    flat = filters.transpose(1, 2, 3, 0).reshape(A_TAPS * B_TAPS, K, NLAT)
    sel_f, sel_b, perm, edge = [jnp.asarray(v) for v in constants()]
    vspec = pl.BlockSpec(memory_space=pltpu.VMEM)
    anyspec = pl.BlockSpec(memory_space=pl.ANY)
    dma = pltpu.SemaphoreType.DMA
    vm = pltpu.VMEM
    scratch = [
        pltpu.SMEM((NLAT,), jnp.int32),
        vm((M, 6, OWN, C), BF16),
        vm((M, 6, OWN, C), BF16),
        vm((6, SIDES, C), BF16),
        vm((6, SIDES, C), BF16),
        vm((2, 2, PAIRS, 16, C), BF16),
        vm((TOK, C), BF16),
        vm((K * C, C), BF16),
        vm((C, FF), BF16),
        vm((FF, C), BF16),
        vm((A_TAPS * B_TAPS, K, NLAT), BF16),
        vm((NF, NLAT), F32),
        vm((NF, K * 256), BF16),
        vm((NF, K * 256), BF16),
        vm((2, 256, M * 256), BF16),
        vm((2 * PAIRS * 16, TOK), BF16),
        vm((16, K * 256), F32),
        vm((8, K * 256), F32),
        vm((2, PAIRS * 96, 256), BF16),
        vm((M, PAIRS, 192, 256), BF16),
        vm((M, PAIRS, 192, 256), BF16),
        vm((TOK, K * C), BF16),
        vm((TOK, FF), F32),
        vm((TOK, FF), F32),
        vm((TOK, FF), BF16),
        vm((TOK, FF), BF16),
        vm((TOK, C), BF16),
        vm((TOK, C), BF16),
        vm((4, 2, 4, 4, 16, C), BF16),
        vm((4, 4, 4, 16, C), BF16),
        vm((4, 4, 4, 16, C), BF16),
        vm((4, 15, 16, C), BF16),
        vm((4, 8, 16, C), BF16),
        vm((4, 2, 4, 4, 16, C), BF16),
        dma((11,)),
        dma((2, 8)),
        dma((2, 8)),
        dma((4,)),
        dma((4,)),
        dma((4,)),
        dma((4,)),
        dma((4,)),
        dma((4,)),
        dma((4,)),
        dma((4,)),
        dma((4,)),
        dma((4,)),
        pltpu.SemaphoreType.REGULAR,
        pltpu.SemaphoreType.REGULAR,
    ]
    results = (((TOK, C), BF16), ((TOK, C), BF16), ((K * C, C), F32), ((C, FF), F32), ((FF, C), F32))
    inner = pl.pallas_call(
        kernel,
        out_shape=[vm(*r) for r in results],
        in_specs=[pl.BlockSpec(memory_space=pltpu.HBM)] * 11,
        out_specs=[vspec] * 5,
        scratch_shapes=scratch,
        compiler_params=pltpu.CompilerParams(
            collective_id=0, has_side_effects=True, vmem_limit_bytes=60 * 2**20
        ),
    )(
        lon_width,
        fields.reshape(M, PAIRS, 48, C),
        cotangent.reshape(TOK, C),
        disco_weight.reshape(K * C, C),
        up_weight,
        down_weight,
        flat,
        sel_f,
        sel_b,
        perm,
        edge,
    )
    out, back, disco, up, down = pl.pallas_call(
        finish,
        out_shape=[jax.ShapeDtypeStruct(*r) for r in results],
        in_specs=[vspec] * 5,
        out_specs=[pl.BlockSpec(memory_space=pltpu.HBM)] * 5,
        scratch_shapes=[dma((5,))],
        compiler_params=pltpu.CompilerParams(vmem_limit_bytes=16 * 2**20),
    )(*[pltpu.with_memory_space_constraint(v, pltpu.VMEM) for v in inner])
    shape = fields.shape
    return out.reshape(shape), back.reshape(shape), disco.reshape(K, C, C), up, down


def solution(mesh):
    placed = (P(None, "lat", "lon", None), P(), P(), P(), P(), P(), P(None, "lat", "lon", None))
    return jax.shard_map(
        per_device,
        mesh=mesh,
        in_specs=placed,
        out_specs=(P(None, "lat", "lon", None), P(None, "lat", "lon", None), P(), P(), P()),
        check_vma=False,
    )
```

```python
import functools

import jax
import jax.numpy as jnp
import numpy as np
from jax import lax
from jax.experimental import pallas as pl
from jax.experimental.pallas import tpu as pltpu
from jax.sharding import PartitionSpec as P

GELU_SCALE = 0.7978845608028654
GELU_CUBE = 0.044715
MESH = pl.DeviceIdType.MESH
F32 = jnp.float32
BF16 = jnp.bfloat16

M, ROWS, CELLS, C, FF, K = 2, 8, 24, 256, 512, 4
NLAT = 64
A_TAPS, B_TAPS = 5, 9
PAIRS = ROWS // 2
TOK = M * ROWS * CELLS
OWN, SIDES = 48, 32
NK = 3 * (OWN + SIDES)
NF = A_TAPS * B_TAPS * 8
PLANE = [(2, 2), (2, 1), (1, 2), (2, 3), (3, 2), (1, 1), (3, 3), (1, 3), (3, 1), (2, 0), (0, 2), (1, 0), (0, 1), (3, 0), (0, 3)]
RING = (4, 3, 5, 2, 6, 1, 7)


def constants():
    sel_f = np.zeros((NF, K * 256), np.float32)
    sel_b = np.zeros((NF, K * 256), np.float32)
    for a in range(A_TAPS):
        for b in range(B_TAPS):
            for k in range(K):
                s = (a * B_TAPS + b) * 8 + k
                sel_f[s, k * 256 + a * 32 + b] = 1
                sel_b[s, k * 256 + (4 - a) * 32 + 8 - b] = 1
    perm = np.zeros((2, 256, M * 256), np.float32)
    for i2 in range(2):
        for a in range(A_TAPS):
            p, r2 = divmod(i2 + a, 2)
            for jj in range(32):
                for m in range(M):
                    side = 3 * OWN + p * SIDES + m * 8 + r2 * 4
                    if jj < 4:
                        col = side + jj
                    elif jj < 28:
                        col = p * OWN + r2 * CELLS + jj - 4
                    else:
                        col = side + 16 + jj - 28
                    perm[i2, a * 32 + jj, m * 256 + col] = 1
    edge = np.zeros((2 * PAIRS * 16, TOK), np.float32)
    for side in range(2):
        for q in range(PAIRS):
            for m in range(M):
                for r2 in range(2):
                    for j in range(4):
                        cell = (CELLS - 4 + j) if side == 0 else j
                        token = ((m * PAIRS + q) * 2 + r2) * CELLS + cell
                        edge[(side * PAIRS + q) * 16 + m * 8 + r2 * 4 + j, token] = 1
    return [x.astype(jnp.bfloat16) for x in (sel_f, sel_b, perm, edge)]


def dot(a, b, dims=((1,), (0,))):
    return lax.dot_general(a, b, (dims, ((), ())), preferred_element_type=F32)


def kernel(
    width, fields, cot, disco, up, down, filt, sel_f, sel_b, perm, edge,
    vout, vback, disco_out, up_out, down_out,
    lw, x, y, xs, ys, stage, vcot, vdisco, vup, vdown, vfilt, filt8, vself, vselb, vperm, vedge,
    vline, lines, band, tap_f, tap_b, spread, pre, cd, hidden, bpre, resid, bres,
    g, rc, a1, r1, rz, o,
    lsem, hs, hr, cs, cr, s1s, s1r, zs, zr, g1s, g1r, gcs, gcr, vouch1, vouch2,
):
    lat, lon = lax.axis_index("lat"), lax.axis_index("lon")
    x_hi, yy = lat // 4, lat % 4
    zz, x_lo, core = lon // 4, (lon // 2) % 2, lon % 2
    xx = x_hi * 2 + x_lo

    def at_xy(dx, dy):
        v = (xx + dx) % 4
        return ((v // 2) * 4 + (yy + dy) % 4, zz * 4 + (v % 2) * 2 + core)

    def at_z(d):
        return (lat, ((zz + d) % 8) * 4 + x_lo * 2 + core)

    pair = (lat, zz * 4 + x_lo * 2 + (1 - core))
    right, left = (lon + 1) % 32, (lon + 31) % 32
    has_up, has_down = lat > 0, lat < 7

    loads = [
        pltpu.make_async_copy(fields, x.at[:, 1:5], lsem.at[0]),
        pltpu.make_async_copy(edge, vedge, lsem.at[1]),
        pltpu.make_async_copy(filt, vfilt, lsem.at[2]),
        pltpu.make_async_copy(sel_f, vself, lsem.at[3]),
        pltpu.make_async_copy(perm, vperm, lsem.at[4]),
        pltpu.make_async_copy(cot, vcot, lsem.at[5]),
        pltpu.make_async_copy(down, vdown, lsem.at[6]),
        pltpu.make_async_copy(disco, vdisco, lsem.at[7]),
        pltpu.make_async_copy(up, vup, lsem.at[8]),
        pltpu.make_async_copy(sel_b, vselb, lsem.at[9]),
        pltpu.make_async_copy(width, lw, lsem.at[10]),
    ]
    loads[0].start()
    loads[1].start()

    barrier = pltpu.get_barrier_semaphore()

    def hello(dev):
        pl.semaphore_signal(barrier, inc=1, device_id=dev, device_id_type=MESH)

    hello((lat, right))
    hello((lat, left))

    @pl.when(has_up)
    def _():
        for v in (left, lon, right):
            hello((lat - 1, v))

    @pl.when(has_down)
    def _():
        for v in (left, lon, right):
            hello((lat + 1, v))

    near_chips = [at_xy(dx, dy) for dx, dy in PLANE if dx != 2 and dy != 2] + [at_z(1), at_z(7)]
    for dev in near_chips:
        hello(dev)

    for c in loads[2:]:
        c.start()

    def clear(n):
        for buf, sides in ((x, xs), (y, ys)):
            buf[:, n] = jnp.zeros((M, OWN, C), BF16)
            sides[n] = jnp.zeros((SIDES, C), BF16)

    @pl.when(lat == 0)
    def _():
        clear(0)

    @pl.when(lat == 7)
    def _():
        clear(5)

    def rdma(src, dst, ss, rs, dev):
        return pltpu.make_async_remote_copy(
            src_ref=src, dst_ref=dst, send_sem=ss, recv_sem=rs, device_id=dev, device_id_type=MESH
        )

    def halo(buf, sides, ph):
        st = stage.at[ph]

        def lon_copies():
            return [
                rdma(st.at[0], sides.at[1:5, 0:16], hs.at[ph, 0], hr.at[ph, 0], (lat, right)),
                rdma(st.at[1], sides.at[1:5, 16:32], hs.at[ph, 1], hr.at[ph, 1], (lat, left)),
            ]

        def to_down():
            return [
                rdma(buf.at[:, 4], buf.at[:, 0], hs.at[ph, 2], hr.at[ph, 2], (lat + 1, lon)),
                rdma(st.at[0, 3], sides.at[0, 0:16], hs.at[ph, 3], hr.at[ph, 3], (lat + 1, right)),
                rdma(st.at[1, 3], sides.at[0, 16:32], hs.at[ph, 4], hr.at[ph, 4], (lat + 1, left)),
            ]

        def to_up():
            return [
                rdma(buf.at[:, 1], buf.at[:, 5], hs.at[ph, 5], hr.at[ph, 5], (lat - 1, lon)),
                rdma(st.at[0, 0], sides.at[5, 0:16], hs.at[ph, 6], hr.at[ph, 6], (lat - 1, right)),
                rdma(st.at[1, 0], sides.at[5, 16:32], hs.at[ph, 7], hr.at[ph, 7], (lat - 1, left)),
            ]

        def start():
            @pl.when(has_down)
            def _():
                for c in to_down():
                    c.start()

            @pl.when(has_up)
            def _():
                for c in to_up():
                    c.start()

            for c in lon_copies():
                c.start()

        def recv():
            for c in lon_copies():
                c.wait_recv()

            @pl.when(has_up)
            def _():
                for c in to_down():
                    c.wait_recv()

            @pl.when(has_down)
            def _():
                for c in to_up():
                    c.wait_recv()

        def sent():
            for c in lon_copies():
                c.wait_send()

            @pl.when(has_down)
            def _():
                for c in to_down():
                    c.wait_send()

            @pl.when(has_up)
            def _():
                for c in to_up():
                    c.wait_send()

        return start, recv, sent

    halo_x = halo(x, xs, 0)
    halo_y = halo(y, ys, 1)

    def own(buf, m):
        return buf[m, 1:5].reshape(ROWS * CELLS, C)

    def fill_stage(buf, ph):
        e = dot(vedge[...], buf[:, 1:5].reshape(TOK, C)).astype(BF16)
        stage[ph] = e.reshape(2, PAIRS, 16, C)

    loads[0].wait()
    loads[1].wait()
    fill_stage(x, 0)
    pl.semaphore_wait(
        barrier, 12 + 3 * has_up.astype(jnp.int32) + 3 * has_down.astype(jnp.int32)
    )
    halo_x[0]()

    def vouch(sem, devs):
        for dev in devs:
            pl.semaphore_signal(sem, inc=1, device_id=dev, device_id_type=MESH)

    vouch(vouch1, near_chips)

    loads[2].wait()
    loads[10].wait()
    filt8[...] = jnp.zeros_like(filt8)
    for n in range(A_TAPS * B_TAPS):
        filt8[n * 8 : n * 8 + K] = vfilt[n].astype(F32)
    first = lat * ROWS - 2
    row_sel = (
        lax.broadcasted_iota(jnp.int32, (16, NLAT), 1)
        == lax.broadcasted_iota(jnp.int32, (16, NLAT), 0) + first
    )
    near = dot(jnp.where(row_sel, 1.0, 0.0).astype(BF16), filt8[...].astype(BF16), ((1,), (1,))).astype(BF16)
    line_row = lax.broadcasted_iota(jnp.int32, (16, K * 256), 0)
    reach = jnp.zeros((16, K * 256), jnp.int32)
    for r in range(12):
        reach = jnp.where(line_row == r, lw[jnp.clip(first + r, 0, NLAT - 1)], reach)
    lane = lax.broadcasted_iota(jnp.int32, (16, K * 256), 1)
    keep = jnp.abs((lane & 31) - 4) <= reach

    def bands(get_line, tap):
        for i in range(ROWS):
            q, i2 = divmod(i, 2)
            parts = []
            for k in range(K):
                line = jnp.broadcast_to(get_line(i, k), (CELLS, 256))
                parts.append(
                    jnp.concatenate(
                        [
                            pltpu.roll(line[:, h * 128 : (h + 1) * 128], 0, 1, stride=1, stride_axis=0)
                            for h in range(2)
                        ],
                        axis=1,
                    )
                )
            band[i2, q * 96 : (q + 1) * 96] = jnp.concatenate(parts, axis=0).astype(BF16)
        res = [dot(band[i2], vperm[i2]) for i2 in range(2)]
        for q in range(PAIRS):
            for k in range(K):
                at = q * 96 + k * CELLS
                both = jnp.concatenate([res[0][at : at + CELLS], res[1][at : at + CELLS]], axis=0)
                for m in range(M):
                    tap[m, q, k * 48 : (k + 1) * 48] = both[:, m * 256 : (m + 1) * 256].astype(BF16)

    loads[3].wait()
    loads[4].wait()
    vline[...] = jnp.where(keep, dot(near, vself[...]), 0.0)
    bands(lambda i, k: vline[i + 2 : i + 3, k * 256 : (k + 1) * 256], tap_f)

    loads[5].wait()
    loads[6].wait()
    cd[...] = dot(vcot[...], vdown[...], ((1,), (1,)))
    loads[9].wait()
    loads[7].wait()
    loads[8].wait()

    def stencil(tap, buf, sides, dst):
        for q in range(PAIRS):
            for m in range(M):
                window = jnp.concatenate(
                    [buf[m, q : q + 3].reshape(3 * OWN, C), sides[q : q + 3].reshape(3 * SIDES, C)], axis=0
                )
                res = dot(tap[m, q][:, :NK], window).astype(BF16)
                for k in range(K):
                    at = m * 192 + q * 48
                    dst[at : at + 48, k * C : (k + 1) * C] = res[k * 48 : (k + 1) * 48]

    halo_x[1]()
    stencil(tap_f, x, xs, spread)

    for m in range(M):
        mixed = dot(spread[m * 192 : (m + 1) * 192], vdisco[...])
        resid[m * 192 : (m + 1) * 192] = (own(x, m).astype(F32) + mixed).astype(BF16)
    pre[...] = dot(resid[...], vup[...])

    @pl.loop(0, TOK // 16)
    def _(n):
        at = pl.ds(pl.multiple_of(n * 16, 16), 16)
        p = pre[at]
        pp = p * p
        t = jnp.tanh(GELU_SCALE * p * (1.0 + GELU_CUBE * pp))
        h = 0.5 * (1.0 + t)
        hidden[at] = (p * h).astype(BF16)
        slope = h + 0.5 * p * (1.0 - t * t) * GELU_SCALE * (1.0 + 3.0 * GELU_CUBE * pp)
        bpre[at] = (cd[at] * slope).astype(BF16)

    rows0 = ((0,), (0,))

    def put(n, value):
        g[n] = value.astype(BF16).reshape(2, 4, 4, 16, C)

    def core_copy(n):
        return rdma(g.at[n, 1 - core], rc.at[n], cs.at[n], cr.at[n], pair)

    put(0, dot(hidden[...], vcot[...], rows0))
    core_copy(0).start()
    gu = dot(resid[...], bpre[...], rows0)
    put(1, jnp.concatenate([gu[:, :C], gu[:, C:]], axis=0))
    core_copy(1).start()

    def plane_copies(n):
        return [
            rdma(
                a1.at[n, (xx + dx) % 4, (yy + dy) % 4], r1.at[n, i], s1s.at[n], s1r.at[n],
                at_xy(dx, dy),
            )
            for i, (dx, dy) in enumerate(PLANE)
        ]

    def z_copies(n):
        ref = rz.at[n, zz]
        return [rdma(ref, ref, zs.at[n], zr.at[n], at_z(d)) for d in RING]

    def gather_copies(n):
        ref = o.at[n, core, xx, yy]
        return [
            rdma(ref, ref, g1s.at[n], g1r.at[n], at_xy(dx, dy))
            for dx, dy in PLANE
        ]

    def gc_copy(n):
        ref = o.at[n, core]
        return rdma(ref, ref, gcs.at[n], gcr.at[n], pair)

    def start(copies):
        for c in copies:
            c.start()

    def wait_all(blocks, sem):
        ref = r1.at[0, 0:blocks]
        pltpu.make_async_copy(ref, ref, sem).wait()

    def do_core(n):
        core_copy(n).wait_recv()
        a1[n] = (g[n, core].astype(F32) + rc[n].astype(F32)).astype(BF16)
        start(plane_copies(n))

    def do_plane(n):
        wait_all(15, s1r.at[n])
        v = a1[n, xx, yy].astype(F32)
        for d in range(15):
            v = v + r1[n, d].astype(F32)
        rz[n, zz] = v.astype(BF16)
        start(z_copies(n))

    def do_z(n):
        wait_all(7, zr.at[n])
        v = rz[n, 0].astype(F32)
        for d in range(1, 8):
            v = v + rz[n, d].astype(F32)
        o[n, core, xx, yy] = v.astype(BF16)
        start(gather_copies(n))

    def do_gather(n):
        wait_all(15, g1r.at[n])
        gc_copy(n).start()

    br = (vcot[...].astype(F32) + dot(bpre[...], vup[...], ((1,), (1,)))).astype(BF16)
    bres[...] = br
    for m in range(M):
        y[m, 1:5] = br[m * 192 : (m + 1) * 192].reshape(PAIRS, 48, C)
    fill_stage(y, 1)
    pl.semaphore_wait(vouch1, 10)
    vouch(vouch2, [at_z(2), at_z(6)])
    do_core(0)
    do_core(1)
    for n in range(2):
        put(2 + n, dot(spread[:, n * 512 : (n + 1) * 512], bres[...], rows0))
        core_copy(2 + n).start()

    do_core(2)
    do_core(3)
    halo_y[0]()
    vline[...] = jnp.where(keep, dot(near, vselb[...]), 0.0)
    group = (lax.broadcasted_iota(jnp.int32, (8, K * 256), 1) // 32) % 8
    total = jnp.zeros((8, K * 256), F32)
    for r in range(A_TAPS):
        total = total + jnp.where(group == r, vline[r : r + 8], 0.0)
    lines[...] = total
    bands(lambda i, k: lines[i : i + 1, k * 256 : (k + 1) * 256], tap_b)

    pl.semaphore_wait(vouch2, 2)
    for n in range(4):
        do_plane(n)

    vout[...] = (resid[...].astype(F32) + dot(hidden[...], vdown[...])).astype(BF16)
    halo_x[2]()
    halo_y[2]()
    for n in range(4):
        core_copy(n).wait_send()
        wait_all(15, s1s.at[n])
    for n in range(4):
        do_z(n)
    for n in range(4):
        wait_all(7, zs.at[n])
    halo_y[1]()
    stencil(tap_b, y, ys, spread)
    for m in range(M):
        at = slice(m * 192, (m + 1) * 192)
        acc = bres[at].astype(F32)
        for k in range(K):
            acc = acc + dot(
                spread[at, k * C : (k + 1) * C], vdisco[k * C : (k + 1) * C], ((1,), (1,))
            )
        vback[at] = acc.astype(BF16)

    for n in range(4):
        do_gather(n)

    for n in range(4):
        wait_all(15, g1s.at[n])
    for n in range(4):
        gc_copy(n).wait_recv()
        whole = o[n].astype(F32)
        if n == 0:
            down_out[...] = whole.reshape(FF, C)
        elif n == 1:
            up_out[:, :C] = whole[0].reshape(C, C)
            up_out[:, C:] = whole[1].reshape(C, C)
        else:
            disco_out[(n - 2) * 512 : (n - 1) * 512] = whole.reshape(512, C)
    for n in range(4):
        gc_copy(n).wait_send()


def finish(*refs):
    sem = refs[10]
    copies = [pltpu.make_async_copy(refs[n], refs[5 + n], sem.at[n]) for n in (2, 3, 4, 0, 1)]
    for c in copies:
        c.start()
    for c in copies:
        c.wait()


def per_device(fields, filters, lon_width, disco_weight, up_weight, down_weight, cotangent):
    flat = filters.transpose(1, 2, 3, 0).reshape(A_TAPS * B_TAPS, K, NLAT)
    sel_f, sel_b, perm, edge = [jnp.asarray(v) for v in constants()]
    vspec = pl.BlockSpec(memory_space=pltpu.VMEM)
    anyspec = pl.BlockSpec(memory_space=pl.ANY)
    dma = pltpu.SemaphoreType.DMA
    vm = pltpu.VMEM
    scratch = [
        pltpu.SMEM((NLAT,), jnp.int32),
        vm((M, 6, OWN, C), BF16),
        vm((M, 6, OWN, C), BF16),
        vm((6, SIDES, C), BF16),
        vm((6, SIDES, C), BF16),
        vm((2, 2, PAIRS, 16, C), BF16),
        vm((TOK, C), BF16),
        vm((K * C, C), BF16),
        vm((C, FF), BF16),
        vm((FF, C), BF16),
        vm((A_TAPS * B_TAPS, K, NLAT), BF16),
        vm((NF, NLAT), F32),
        vm((NF, K * 256), BF16),
        vm((NF, K * 256), BF16),
        vm((2, 256, M * 256), BF16),
        vm((2 * PAIRS * 16, TOK), BF16),
        vm((16, K * 256), F32),
        vm((8, K * 256), F32),
        vm((2, PAIRS * 96, 256), BF16),
        vm((M, PAIRS, 192, 256), BF16),
        vm((M, PAIRS, 192, 256), BF16),
        vm((TOK, K * C), BF16),
        vm((TOK, FF), F32),
        vm((TOK, FF), F32),
        vm((TOK, FF), BF16),
        vm((TOK, FF), BF16),
        vm((TOK, C), BF16),
        vm((TOK, C), BF16),
        vm((4, 2, 4, 4, 16, C), BF16),
        vm((4, 4, 4, 16, C), BF16),
        vm((4, 4, 4, 16, C), BF16),
        vm((4, 15, 16, C), BF16),
        vm((4, 8, 16, C), BF16),
        vm((4, 2, 4, 4, 16, C), BF16),
        dma((11,)),
        dma((2, 8)),
        dma((2, 8)),
        dma((4,)),
        dma((4,)),
        dma((4,)),
        dma((4,)),
        dma((4,)),
        dma((4,)),
        dma((4,)),
        dma((4,)),
        dma((4,)),
        dma((4,)),
        pltpu.SemaphoreType.REGULAR,
        pltpu.SemaphoreType.REGULAR,
    ]
    results = (((TOK, C), BF16), ((TOK, C), BF16), ((K * C, C), F32), ((C, FF), F32), ((FF, C), F32))
    inner = pl.pallas_call(
        kernel,
        out_shape=[vm(*r) for r in results],
        in_specs=[pl.BlockSpec(memory_space=pltpu.HBM)] * 11,
        out_specs=[vspec] * 5,
        scratch_shapes=scratch,
        compiler_params=pltpu.CompilerParams(
            collective_id=0, has_side_effects=True, vmem_limit_bytes=60 * 2**20
        ),
    )(
        lon_width,
        fields.reshape(M, PAIRS, 48, C),
        cotangent.reshape(TOK, C),
        disco_weight.reshape(K * C, C),
        up_weight,
        down_weight,
        flat,
        sel_f,
        sel_b,
        perm,
        edge,
    )
    out, back, disco, up, down = pl.pallas_call(
        finish,
        out_shape=[jax.ShapeDtypeStruct(*r) for r in results],
        in_specs=[vspec] * 5,
        out_specs=[pl.BlockSpec(memory_space=pltpu.HBM)] * 5,
        scratch_shapes=[dma((5,))],
        compiler_params=pltpu.CompilerParams(vmem_limit_bytes=16 * 2**20),
    )(*[pltpu.with_memory_space_constraint(v, pltpu.VMEM) for v in inner])
    shape = fields.shape
    return out.reshape(shape), back.reshape(shape), disco.reshape(K, C, C), up, down


def solution(mesh):
    placed = (P(None, "lat", "lon", None), P(), P(), P(), P(), P(), P(None, "lat", "lon", None))
    return jax.shard_map(
        per_device,
        mesh=mesh,
        in_specs=placed,
        out_specs=(P(None, "lat", "lon", None), P(None, "lat", "lon", None), P(), P(), P()),
        check_vma=False,
    )
```
